512 devices in a mesh: dp: 64 (over y_lo, z, core), neg: 8 (over y_hi, x).
Axes of the slice: x: 4, y: 8 (y_hi: 2, y_lo: 4; y = y_hi * 4 + y_lo), z: 8, core: 2. Of those that a mesh axis runs over, the one named last changes fastest.
Arguments:
- queries: bfloat16 [131072, 256], P(('dp', 'neg')), may hold values from -6 to 6
- positives: bfloat16 [131072, 256], P(('dp', 'neg')), may hold values from -5 to 5
- negatives: bfloat16 [16384, 256], P('neg'), may hold values from -4.5 to 4.5
- pos_ids: int32 [131072], P(('dp', 'neg')), may hold values from 0 to 65535
- neg_ids: int32 [16384], P('neg'), may hold values from 0 to 65535
- counts: int32 [65536], replicated, may hold values from 1 to 1023
Outputs:
- query_grad: float32 [131072, 256], P(('dp', 'neg'))
- row_loss: float32 [131072], P(('dp', 'neg'))
- neg_grad: float32 [16384, 256], P(('neg', 'dp'))
The draws below stay inside these ranges and needn't reach their ends.
All inputs are finite; a program needn't handle non-finite values.
Results may differ from the reference program's by a relative error of at most 0.0014.
Values may be sent and summed in bfloat16 or wider, within the bound.
No kernel may reach another device: no remote copies, remote signals or barrier semaphores. Data moves between devices by JAX's collectives and lax.ppermute only.
A program may use at most 64 MiB of HBM per device.

```python
import math
import jax
import jax.numpy as jnp
import numpy as np
from jax import lax

D = 256
NNEG = 16384
ITEMS = 65536
TOKENS = 131072


def draw_queries(key, part):
    key = jax.random.fold_in(key, 11)
    return (jnp.clip(jax.random.normal(key, (TOKENS, D), jnp.float32), -5.0, 5.0) / 4.0).astype(jnp.bfloat16)


def draw_negatives(key, part):
    key = jax.random.fold_in(key, 23)
    return jnp.clip(jax.random.normal(key, (NNEG, D), jnp.float32), -4.0, 4.0).astype(jnp.bfloat16)


def plant(entries, own_key, smallest, high):
    longest = entries.shape.index(max(entries.shape))
    spots = []
    for shift in (0, 1):
        where = [jax.random.randint(jax.random.fold_in(own_key, axis), (), 0, length) for axis, length in enumerate(entries.shape)]
        where[longest] = (where[longest] + shift) % entries.shape[longest]
        spots.append(tuple(where))
    return entries.at[spots[0]].set(smallest).at[spots[1]].set(high)


def level_of(key, dims, pieces, low, largest):
    factor_of = 1.0
    for dim, parts in pieces:
        heights = jax.random.uniform(jax.random.fold_in(jax.random.fold_in(key, 6), dim), (parts,), jnp.float32, low / len(pieces), largest / len(pieces))
        factor_of = factor_of * jnp.repeat(jnp.exp(heights), dims[dim] // parts).reshape((-1,) + (1,) * (len(dims) - 1 - dim))
    return factor_of


def cumulative_ranks(count, skew):
    loads = [(1 << 20) // math.isqrt(standing ** skew) + 1 for standing in range(1, count + 1)]
    spread = 1 + sum(loads) // (1 << 30)
    return np.cumsum(np.array([max(1, weight // spread) for weight in loads]))


def ranked_ids(stream_key, dims, amount, slope):
    grid = cumulative_ranks(amount, slope)
    ticket = jax.random.randint(jax.random.fold_in(stream_key, 1), dims, 0, int(grid[amount - 1]))
    standing = jnp.searchsorted(jnp.asarray(grid, jnp.int32), ticket, side="right")
    return jax.random.permutation(jax.random.fold_in(stream_key, 2), amount)[standing].astype(jnp.int32)


def centred(key, shape, deviation, most, pieces=(), held_as=jnp.bfloat16):
    drawn = jax.random.normal(key, shape, jnp.float32) * deviation
    if len(pieces) > 0:
        drawn = level_of(key, shape, pieces, -0.22, 0.18) * drawn
    return jnp.clip(drawn, min=-most, max=most).astype(held_as)


def setup_inputs(seed: int = 0) -> dict:
    seeds = jax.random.split(jax.random.key(seed), 7)
    return {
        "queries": draw_queries(jax.random.fold_in(seeds[6], 71), 0),
        "positives": centred(seeds[1], (TOKENS, D), 1.0, 5.0, ((0, 512),)),
        "negatives": draw_negatives(jax.random.fold_in(seeds[6], 71), 0),
        "pos_ids": plant(ranked_ids(seeds[3], (TOKENS,), ITEMS, 2), jax.random.fold_in(seeds[3], 3), 0, ITEMS - 1).astype(jnp.int32),
        "neg_ids": plant(ranked_ids(seeds[4], (NNEG,), ITEMS, 2), jax.random.fold_in(seeds[4], 3), 0, ITEMS - 1).astype(jnp.int32),
        "counts": plant(jax.random.randint(seeds[5], (ITEMS,), 1, 1024), jax.random.fold_in(seeds[5], 1), 1, 1023).astype(jnp.int32),
    }


def reference(queries, positives, negatives, pos_ids, neg_ids, counts):
    correction = jnp.log(counts.astype(jnp.float32))
    neg_corr = correction[neg_ids]
    pos_corr = correction[pos_ids]
    neg_float = negatives.astype(jnp.float32)
    row_block = min(1024, TOKENS)
    nblocks = TOKENS // row_block
    query_blocks = queries.reshape(nblocks, row_block, D)
    pos_blocks = positives.reshape(nblocks, row_block, D)
    corr_blocks = pos_corr.reshape(nblocks, row_block)

    def handle(total, inputs):
        query_part, pos_part, corr_part = inputs
        query_float = query_part.astype(jnp.float32)
        pos_float = pos_part.astype(jnp.float32)
        pos_score = jnp.sum(query_float * pos_float, axis=1) - corr_part
        logits = jnp.dot(query_float, neg_float.T, precision=lax.Precision.HIGHEST) - neg_corr[None, :]
        row_max = jnp.maximum(jnp.max(logits, axis=1), pos_score)
        row_sum = jnp.sum(jnp.exp(logits - row_max[:, None]), axis=1) + jnp.exp(pos_score - row_max)
        lse = row_max + jnp.log(row_sum)
        weight = jnp.exp(logits - lse[:, None]).astype(jnp.bfloat16)
        pos_weight = jnp.exp(pos_score - lse)
        weight_float = weight.astype(jnp.float32)
        grad_rows = jnp.dot(weight_float, neg_float, precision=lax.Precision.HIGHEST) + (pos_weight - 1.0)[:, None] * pos_float
        total = total + jnp.dot(weight_float.T, query_float, precision=lax.Precision.HIGHEST)
        return total, (grad_rows, lse - pos_score)

    start = jnp.zeros((NNEG, D), jnp.float32)
    neg_grad, (grad_rows, losses) = lax.scan(handle, start, (query_blocks, pos_blocks, corr_blocks))
    return grad_rows.reshape(TOKENS, D), losses.reshape(TOKENS), neg_grad
```

```python
import jax
import jax.numpy as jnp
from jax import lax
from jax.experimental import pallas as pl
from jax.experimental.pallas import tpu as pltpu
from jax.sharding import PartitionSpec as P

LANES = 128
CHUNK = 512
SPAN = 60.0
VMEM_BYTES = 48 * 1024 * 1024
FAR, NEAR = 2, 4
LINE, RING, CORES = 4, 8, 2


def dot(a, b, dims):
    return lax.dot_general(a, b, (dims, ((), ())), preferred_element_type=jnp.float32)


def params():
    return pltpu.CompilerParams(vmem_limit_bytes=VMEM_BYTES)


def cost(flops, nbytes, exps):
    return pl.CostEstimate(flops=flops, bytes_accessed=nbytes, transcendentals=exps)


def mirror(value):
    perm = []
    for l in range(LINE):
        for g in range(RING * CORES):
            for n in range(FAR * NEAR):
                to = ((LINE - 1 - l) * RING * CORES + g) * FAR * NEAR + (n + NEAR) % (FAR * NEAR)
                perm.append(((l * RING * CORES + g) * FAR * NEAR + n, to))
    return lax.ppermute(value, ("dp", "neg"), perm)


def other_core(value):
    perm = [(index, index ^ 1) for index in range(LINE * RING * CORES)]
    return lax.ppermute(value, "dp", perm)


def lookup_kernel(
    place_ref, counts_ref, neg_ids_ref, pos_ids_ref, queries_ref, pos_ref, negatives_ref,
    corr_ref, score_ref, order_ref,
):
    counts = counts_ref[...].astype(jnp.float32)
    high = jnp.floor(counts * 0.125)
    digits = jnp.concatenate([high, counts - 8.0 * high], axis=1)
    table = digits.T.astype(jnp.bfloat16)
    table_rows = counts_ref.shape[0]
    total = negatives_ref.shape[0]
    block = total // (LINE * RING * CORES)
    place = place_ref[0]
    core = place & (CORES - 1)

    def corrections(ids):
        row = ids >> 7
        column = ids & (LANES - 1)
        width = ids.shape[1]
        spots = lax.broadcasted_iota(jnp.int32, (table_rows, width), 0)
        hot = jnp.where(spots == row, 1.0, 0.0).astype(jnp.bfloat16)
        found = dot(table, hot, ((1,), (0,)))
        value = 8.0 * found[:LANES] + found[LANES:]
        lanes = lax.broadcasted_iota(jnp.int32, (LANES, width), 0)
        picked = jnp.sum(jnp.where(lanes == column, value, 0.0), axis=0, keepdims=True)
        return jnp.log(picked)

    def target(index):
        l, r, c = index // (RING * CORES), (index // CORES) % RING, index % CORES
        away = (c - core) & (CORES - 1)
        return pl.ds(pl.multiple_of((away * LINE + l) * RING * block, block) + r * block, block)

    for k in range(neg_ids_ref.shape[0]):
        corr = corrections(neg_ids_ref[k : k + 1, :])
        tall = jnp.broadcast_to(corr, (LANES, LANES)).T
        for b in range(LANES // block):
            rows = target(k * (LANES // block) + b)
            corr_ref[rows, :] = tall[b * block : (b + 1) * block, :]
    for k in range(total // block):
        order_ref[target(k), :] = negatives_ref[k * block : (k + 1) * block, :]
    products = queries_ref[...].astype(jnp.float32) * pos_ref[...].astype(jnp.float32)
    scores = jnp.sum(products.T, axis=0, keepdims=True)
    for k in range(pos_ids_ref.shape[0]):
        corr = corrections(pos_ids_ref[k : k + 1, :])
        lanes = slice(k * LANES, (k + 1) * LANES)
        score_ref[:, lanes] = scores[:, lanes] - corr


def wide(block, width):
    return jnp.concatenate([block] * (width // LANES), axis=1)


def row_stats(block, negatives_ref, corr_ref):
    rows = block.shape[0]
    top = None
    for start in range(0, negatives_ref.shape[0], CHUNK):
        part = slice(start, start + CHUNK)
        scores = dot(negatives_ref[part, :], block, ((1,), (1,)))
        scores = scores - wide(corr_ref[part, :], rows)
        tiles = scores.reshape(CHUNK // 8, 8, rows)
        best = jnp.max(tiles, axis=0)
        if top is None:
            top = best
            mass = jnp.sum(jnp.exp(tiles - top[None]), axis=0)
        else:
            new = jnp.maximum(top, best)
            mass = mass * jnp.exp(top - new) + jnp.sum(jnp.exp(tiles - new[None]), axis=0)
            top = new
    row_max = jnp.max(top, axis=0, keepdims=True)
    return row_max, jnp.sum(mass * jnp.exp(top - row_max), axis=0, keepdims=True)


def near_stats_kernel(spot_ref, queries_ref, negatives_ref, corr_ref, score_ref, out_ref):
    score = score_ref[...]
    for k in range(NEAR):
        row_max, row_sum = row_stats(queries_ref[k], negatives_ref, corr_ref)
        own = spot_ref[0] == k
        joined = jnp.where(own, jnp.maximum(row_max, score), row_max)
        extra = jnp.exp(jnp.where(own, score, joined) - joined)
        row_sum = row_sum * jnp.exp(row_max - joined) + jnp.where(own, extra, 0.0)
        out_ref[k : k + 1, :] = joined + jnp.log(row_sum)


def far_stats_kernel(queries_ref, negatives_ref, corr_ref, near_ref, out_ref):
    for c in range(NEAR):
        out_ref[c, :NEAR, :] = near_ref[...]
    for k in range(NEAR):
        row_max, row_sum = row_stats(queries_ref[k], negatives_ref, corr_ref)
        lse = row_max + jnp.log(row_sum)
        for c in range(NEAR):
            out_ref[c, NEAR + k : NEAR + k + 1, :] = lse


def join_kernel(parts_ref, out_ref):
    top = parts_ref[0]
    for c in range(1, NEAR):
        top = jnp.maximum(top, parts_ref[c])
    total = jnp.exp(parts_ref[0] - top)
    for c in range(1, NEAR):
        total = total + jnp.exp(parts_ref[c] - top)
    out_ref[...] = top + jnp.log(total)


def grads_kernel(
    spot_ref, near_ref, far_ref, parts_ref, joined_ref, other_ref, negatives_ref, turned_ref,
    corr_ref, query_out, keep_out, send_out, lse_out, share_out,
):
    total = negatives_ref.shape[0]
    spot = spot_ref[0]
    joined = joined_ref[...]
    other = jnp.concatenate([other_ref[NEAR:, :], other_ref[:NEAR, :]], axis=0)
    top = jnp.maximum(joined, other)
    lse_out[...] = top + jnp.log(jnp.exp(joined - top) + jnp.exp(other - top))
    lse_all = lse_out[...]
    local = parts_ref[spot]
    boost = jnp.exp(jnp.minimum(lse_all - local, SPAN))
    own = lse_out[pl.ds(spot, 1), :]
    mirrored = lse_out[pl.ds(spot + NEAR, 1), :]
    sent = jnp.minimum(mirrored - joined_ref[pl.ds(spot + NEAR, 1), :], SPAN)
    for c in range(NEAR):
        part = jnp.minimum(own - parts_ref[c, pl.ds(spot, 1), :], SPAN)
        share_out[c, 0] = jnp.exp(-part)
        part = jnp.minimum(mirrored - parts_ref[c, pl.ds(spot + NEAR, 1), :], SPAN)
        share_out[c, 1] = jnp.exp(sent - part)
    half = total // CORES
    for k in range(FAR * NEAR):
        block = near_ref[k] if k < NEAR else far_ref[k - NEAR]
        rows = block.shape[0]
        lse = lse_all[k : k + 1, :]
        query_total = None
        for start in range(0, total, CHUNK):
            part = slice(start, start + CHUNK)
            scores = dot(negatives_ref[part, :], block, ((1,), (1,)))
            scores = scores - wide(corr_ref[part, :], rows)
            weight = jnp.exp(scores - lse).astype(jnp.bfloat16)
            neg_term = dot(weight, block, ((1,), (0,)))
            out, place = (keep_out, start) if start < half else (send_out, start - half)
            place = slice(place, place + CHUNK)
            if k > 0:
                neg_term = out[place, :] + neg_term
            out[place, :] = neg_term
            term = dot(turned_ref[:, part], weight, ((1,), (0,)))
            query_total = term if query_total is None else query_total + term
        query_out[k % NEAR, k // NEAR] = query_total * boost[k : k + 1, :]


def sum_cores_kernel(keep_ref, got_ref, out_ref):
    total = keep_ref[...] + got_ref[...]
    top = jnp.max(jnp.max(jnp.abs(total), axis=0, keepdims=True), axis=1, keepdims=True)
    power = jnp.clip(jnp.floor(jnp.log2(jnp.maximum(top, 1e-30))), -99.0, 99.0)
    scaled = total * jnp.exp2(13.0 - power)
    count, padded, width = out_ref.shape
    block = total.shape[0] // count
    for k in range(count):
        out_ref[k, :block, :] = scaled[k * block : (k + 1) * block, :]
        out_ref[k, block:, :] = jnp.broadcast_to(power, (padded - block, width))


def finish_kernel(
    spot_ref, own_ref, far_ref, pos_ref, score_ref, lse_ref, other_ref, grad_ref, loss_ref
):
    spot = spot_ref[0]
    lse = lse_ref[pl.ds(spot, 1), :]
    share = jnp.exp(-jnp.minimum(lse - other_ref[pl.ds(spot + NEAR, 1), :], SPAN))
    score = score_ref[...]
    pos_weight = jnp.exp(score - lse)
    turned = own_ref[...] + far_ref[...] * share
    turned = turned + (pos_weight - 1.0) * pos_ref[...].astype(jnp.float32).T
    grad_ref[...] = turned.T
    loss_ref[...] = lse - score


def trade(value, axis, groups):
    return lax.all_to_all(value, axis, 0, 0, tiled=True, axis_index_groups=groups)


def per_device(queries, positives, negatives, pos_ids, neg_ids, counts):
    own, width = queries.shape
    shard = negatives.shape[0]
    parts = FAR * NEAR
    f32, f16 = jnp.float32, jnp.float16
    like = jax.ShapeDtypeStruct
    place = lax.axis_index("dp").astype(jnp.int32).reshape(1)
    spot = (lax.axis_index("neg").astype(jnp.int32) % NEAR).reshape(1)
    smem = pl.BlockSpec(memory_space=pltpu.SMEM)
    vmem = pl.BlockSpec(memory_space=pltpu.VMEM)
    rows = [[f * NEAR + n for n in range(NEAR)] for f in range(FAR)]
    sheets = [[g * CORES + c for g in range(LINE * RING)] for c in range(CORES)]

    def spread(value):
        return trade(jnp.broadcast_to(value[None], (NEAR,) + value.shape), "neg", rows)

    across = mirror(queries)
    near_blocks = spread(queries)
    far_blocks = spread(across)

    corr, score, ordered = pl.pallas_call(
        lookup_kernel,
        in_specs=[smem] + [vmem] * 6,
        out_specs=(vmem, vmem, vmem),
        out_shape=(
            like((shard, LANES), f32),
            like((1, own), f32),
            like((shard, width), jnp.bfloat16),
        ),
        compiler_params=params(),
        cost_estimate=cost(10**9, 2 * 10**6, 4096),
        name="lookup",
    )(
        place,
        counts.reshape(-1, LANES),
        neg_ids.reshape(-1, LANES),
        pos_ids.reshape(-1, LANES),
        queries,
        positives,
        negatives,
    )
    turned = ordered.T

    pairs = parts * own * shard
    near_stats = pl.pallas_call(
        near_stats_kernel,
        in_specs=[smem] + [vmem] * 4,
        out_specs=vmem,
        out_shape=like((NEAR, own), f32),
        compiler_params=params(),
        cost_estimate=cost(pairs * width, 2 * 10**6, pairs // 2),
        name="near_stats",
    )(spot, near_blocks, ordered, corr, score)
    stats = pl.pallas_call(
        far_stats_kernel,
        in_specs=[vmem] * 4,
        out_specs=vmem,
        out_shape=like((NEAR, parts, own), f32),
        compiler_params=params(),
        cost_estimate=cost(pairs * width, 2 * 10**6, pairs // 2),
        name="far_stats",
    )(far_blocks, ordered, corr, near_stats)
    stats = trade(stats, "neg", rows)
    joined = pl.pallas_call(
        join_kernel,
        in_specs=[vmem],
        out_specs=vmem,
        out_shape=like((parts, own), f32),
        compiler_params=params(),
        name="join",
    )(stats)
    other = mirror(joined)

    query_terms, keep, send, lse, share = pl.pallas_call(
        grads_kernel,
        in_specs=[smem] + [vmem] * 8,
        out_specs=(vmem,) * 5,
        out_shape=(
            like((NEAR, FAR, width, own), f32),
            like((shard // CORES, width), f32),
            like((shard // CORES, width), f32),
            like((parts, own), f32),
            like((NEAR, FAR, 1, own), f32),
        ),
        compiler_params=params(),
        cost_estimate=cost(6 * pairs * width, 8 * 10**6, pairs),
        name="grads",
    )(spot, near_blocks, far_blocks, stats, joined, other, ordered, turned, corr)

    query_acc = trade(query_terms.astype(f16), "neg", rows)
    query_acc = jnp.sum(query_acc.astype(f32) * share, axis=0)
    query_far = mirror(query_acc[1].astype(f16)).astype(f32)

    count = LINE * RING
    block = shard // CORES // count
    neg_acc = pl.pallas_call(
        sum_cores_kernel,
        in_specs=[vmem] * 2,
        out_specs=vmem,
        out_shape=like((count, block + 8, width), f32),
        compiler_params=params(),
        name="sum_cores",
    )(keep, other_core(send))
    neg_acc = trade(neg_acc.astype(f16), "dp", sheets).astype(f32)
    power = jnp.exp2(neg_acc[:, block : block + 1, :1] - 13.0)
    neg_grad = jnp.sum(neg_acc[:, :block, :] * power, axis=0)

    query_grad, row_loss = pl.pallas_call(
        finish_kernel,
        in_specs=[smem] + [vmem] * 6,
        out_specs=(vmem, vmem),
        out_shape=(like((own, width), f32), like((1, own), f32)),
        compiler_params=params(),
        name="finish",
    )(spot, query_acc[0], query_far, positives, score, lse, other)
    return (query_grad, row_loss.reshape(own), neg_grad)


def solution(mesh):
    placed = (
        P(("dp", "neg"), None),
        P(("dp", "neg"), None),
        P("neg", None),
        P(("dp", "neg")),
        P("neg"),
        P(),
    )
    return jax.shard_map(
        per_device,
        mesh=mesh,
        in_specs=placed,
        out_specs=(P(("dp", "neg"), None), P(("dp", "neg")), P(("neg", "dp"), None)),
        check_vma=False,
    )
```

```python
import functools
import jax
import jax.numpy as jnp
from jax import lax
from jax.experimental import pallas as pl
from jax.experimental.pallas import tpu as pltpu
from jax.sharding import PartitionSpec as P

LANES = 128
CHUNK = 512
SPLIT = 256
SPAN = 60.0
MIB = 1024 * 1024
FAR, NEAR = 2, 4
HALVING = (3, 1)
LINE, RING, CORES = 4, 8, 2


def dot(a, b, dims):
    return lax.dot_general(a, b, (dims, ((), ())), preferred_element_type=jnp.float32)


def params(mib=16):
    return pltpu.CompilerParams(vmem_limit_bytes=mib * MIB)


def cost(flops, nbytes, exps):
    return pl.CostEstimate(flops=flops, bytes_accessed=nbytes, transcendentals=exps)


def mirror(value):
    perm = []
    for l in range(LINE):
        for g in range(RING * CORES):
            for n in range(FAR * NEAR):
                to = ((LINE - 1 - l) * RING * CORES + g) * FAR * NEAR + (n + NEAR) % (FAR * NEAR)
                perm.append(((l * RING * CORES + g) * FAR * NEAR + n, to))
    return lax.ppermute(value, ("dp", "neg"), perm)


def swap_near(value, bits):
    perm = [(index, index ^ bits) for index in range(FAR * NEAR)]
    return lax.ppermute(value, "neg", perm)


def other_core(value):
    perm = [(index, index ^ 1) for index in range(LINE * RING * CORES)]
    return lax.ppermute(value, "dp", perm)


def lookup_kernel(
    place_ref, counts_ref, neg_ids_ref, pos_ids_ref, queries_ref, pos_ref, negatives_ref,
    corr_ref, score_ref, order_ref, tall_ref,
):
    counts = counts_ref[...].astype(jnp.float32)
    high = jnp.floor(counts * 0.125)
    digits = jnp.concatenate([high, counts - 8.0 * high], axis=1)
    table = digits.T.astype(jnp.bfloat16)
    table_rows = counts_ref.shape[0]
    total = negatives_ref.shape[0]
    block = total // (LINE * RING * CORES)
    place = place_ref[0]
    core = place & (CORES - 1)

    def corrections(ids):
        row = ids >> 7
        column = ids & (LANES - 1)
        width = ids.shape[1]
        spots = lax.broadcasted_iota(jnp.int32, (table_rows, width), 0)
        hot = jnp.where(spots == row, 1.0, 0.0).astype(jnp.bfloat16)
        found = dot(table, hot, ((1,), (0,)))
        value = 8.0 * found[:LANES] + found[LANES:]
        lanes = lax.broadcasted_iota(jnp.int32, (LANES, width), 0)
        picked = jnp.sum(jnp.where(lanes == column, value, 0.0), axis=0, keepdims=True)
        return jnp.log(picked)

    def target(index):
        l, r, c = index // (RING * CORES), (index // CORES) % RING, index % CORES
        away = (c - core) & (CORES - 1)
        return pl.ds(pl.multiple_of((away * LINE + l) * RING * block, block) + r * block, block)

    for k in range(neg_ids_ref.shape[0]):
        corr = corrections(neg_ids_ref[k : k + 1, :])
        tall = jnp.broadcast_to(corr, (LANES, LANES)).T
        for b in range(LANES // block):
            rows = target(k * (LANES // block) + b)
            tall_ref[rows, :] = tall[b * block : (b + 1) * block, :]
    for k in range(total // LANES):
        corr_ref[k : k + 1, :] = tall_ref[k * LANES : (k + 1) * LANES, :].T[:1, :]
    for k in range(total // block):
        order_ref[target(k), :] = negatives_ref[k * block : (k + 1) * block, :]
    products = queries_ref[...].astype(jnp.float32) * pos_ref[...].astype(jnp.float32)
    scores = jnp.sum(products.T, axis=0, keepdims=True)
    for k in range(pos_ids_ref.shape[0]):
        corr = corrections(pos_ids_ref[k : k + 1, :])
        lanes = slice(k * LANES, (k + 1) * LANES)
        score_ref[:, lanes] = scores[:, lanes] - corr


def wide(block, width):
    return jnp.concatenate([block] * (width // LANES), axis=1)


def row_stats(block, negatives_ref, corr_ref):
    rows = block.shape[0]
    top = None
    for start in range(0, negatives_ref.shape[0], CHUNK):
        part = slice(start, start + CHUNK)
        scores = dot(negatives_ref[part, :], block, ((1,), (1,)))
        scores = scores - wide(corr_ref[part, :], rows)
        tiles = scores.reshape(CHUNK // 8, 8, rows)
        best = jnp.max(tiles, axis=0)
        if top is None:
            top = best
            mass = jnp.sum(jnp.exp(tiles - top[None]), axis=0)
        else:
            new = jnp.maximum(top, best)
            mass = mass * jnp.exp(top - new) + jnp.sum(jnp.exp(tiles - new[None]), axis=0)
            top = new
    row_max = jnp.max(top, axis=0, keepdims=True)
    return row_max, jnp.sum(mass * jnp.exp(top - row_max), axis=0, keepdims=True)


def to_columns(rows_ref, out_ref):
    for k in range(rows_ref.shape[0]):
        tall = jnp.broadcast_to(rows_ref[k : k + 1, :], (LANES, LANES)).T
        out_ref[k * LANES : (k + 1) * LANES, :] = tall


def stats_kernel(
    spot_ref, blocks_hbm, negatives_ref, rows_ref, score_ref, out_ref, blocks_ref, corr_ref, sem
):
    fetch = pltpu.make_async_copy(blocks_hbm, blocks_ref, sem)
    fetch.start()
    to_columns(rows_ref, corr_ref)
    fetch.wait()
    score = score_ref[...]
    for side in range(FAR):
        for k in range(NEAR):
            row_max, row_sum = row_stats(blocks_ref[k, side], negatives_ref, corr_ref)
            if side == 0:
                own = spot_ref[0] == k
                joined = jnp.where(own, jnp.maximum(row_max, score), row_max)
                extra = jnp.exp(jnp.where(own, score, joined) - joined)
                row_sum = row_sum * jnp.exp(row_max - joined) + jnp.where(own, extra, 0.0)
                row_max = joined
            lse = row_max + jnp.log(row_sum)
            place = side * NEAR + k
            for c in range(NEAR):
                out_ref[c, place : place + 1, :] = lse


def join(parts):
    top = functools.reduce(jnp.maximum, parts)
    return top + jnp.log(sum(jnp.exp(part - top) for part in parts))


def join_kernel(parts_ref, out_ref):
    out_ref[...] = join([parts_ref[c] for c in range(NEAR)])


def grads_kernel(
    side, spot_ref, blocks_hbm, joined_ref, other_ref, negatives_ref, turned_ref, rows_ref, *refs
):
    sums, refs = refs[: 2 - 2 * side], refs[2 - 2 * side :]
    query_outs, refs = refs[: 2 - side], refs[2 - side :]
    keep_out, send_out, lse_out, boost_ref, weight_ref, blocks_ref, corr_ref, sem = refs
    fetch = pltpu.make_async_copy(blocks_hbm, blocks_ref, sem)
    fetch.start()
    to_columns(rows_ref, corr_ref)
    total = negatives_ref.shape[0]
    spot = spot_ref[0]
    offset = side * NEAR
    joined = joined_ref[offset : offset + NEAR, :]
    lse_all = join([joined, other_ref[NEAR - offset : 2 * NEAR - offset, :]])
    lse_out[...] = lse_all
    boost_ref[...] = jnp.exp(jnp.minimum(lse_all - joined, SPAN))
    places = list(range(NEAR)) if side else [spot ^ k for k in range(NEAR)]
    lse = jnp.concatenate([lse_out[pl.ds(k, 1), :] for k in places], axis=1)
    fetch.wait()
    block = jnp.concatenate([blocks_ref[k, side] for k in places], axis=0)
    rows = block.shape[0]
    own = rows // NEAR
    half = total // CORES
    for start in range(0, total, SPLIT):
        part = slice(start, start + SPLIT)
        scores = dot(negatives_ref[part, :], block, ((1,), (1,)))
        scores = scores - wide(corr_ref[part, :], rows)
        weight = jnp.exp(scores - lse).astype(jnp.bfloat16)
        weight_ref[part, :] = weight
        neg_term = dot(weight, block, ((1,), (0,)))
        which, place = start // half, slice(start % half, start % half + SPLIT)
        if sums:
            neg_term = sums[which][place, :] + neg_term
        (keep_out, send_out)[which][place, :] = neg_term
    first, onward = HALVING
    for index, k in enumerate(places):
        weight = weight_ref[:, index * own : (index + 1) * own]
        term = dot(turned_ref[...], weight, ((1,), (0,))) * boost_ref[pl.ds(k, 1), :]
        if side:
            query_outs[0][index] = term
        else:
            out = query_outs[index in (first, first ^ onward)]
            out[int(index in (onward, first ^ onward))] = term


def spread_kernel(near_ref, far_ref, out_ref):
    for k in range(NEAR):
        out_ref[k, 0] = near_ref[...]
        out_ref[k, 1] = far_ref[...]


def sum_cores_kernel(keep_ref, got_ref, out_ref):
    total = keep_ref[...] + got_ref[...]
    top = jnp.max(jnp.max(jnp.abs(total), axis=0, keepdims=True), axis=1, keepdims=True)
    power = jnp.clip(jnp.floor(jnp.log2(jnp.maximum(top, 1e-30))), -99.0, 99.0)
    scaled = total * jnp.exp2(13.0 - power)
    count, padded, width = out_ref.shape
    block = total.shape[0] // count
    for k in range(count):
        out_ref[k, :block, :] = scaled[k * block : (k + 1) * block, :]
        out_ref[k, block:, :] = jnp.broadcast_to(power, (padded - block, width))


def finish_kernel(
    spot_ref, near_ref, far_ref, pos_ref, score_ref, lse_ref, joined_ref, other_ref,
    grad_ref, loss_ref,
):
    spot = spot_ref[0]
    lse = lse_ref[pl.ds(spot, 1), :]
    near_share = jnp.exp(-jnp.minimum(lse - joined_ref[pl.ds(spot, 1), :], SPAN))
    far_share = jnp.exp(-jnp.minimum(lse - other_ref[pl.ds(spot + NEAR, 1), :], SPAN))
    score = score_ref[...]
    pos_weight = jnp.exp(score - lse)
    turned = near_ref[...] * near_share + far_ref[...] * far_share
    turned = turned + (pos_weight - 1.0) * pos_ref[...].astype(jnp.float32).T
    grad_ref[...] = turned.T
    loss_ref[...] = lse - score


def trade(value, axis, groups):
    return lax.all_to_all(value, axis, 0, 0, tiled=True, axis_index_groups=groups)


def per_device(queries, positives, negatives, pos_ids, neg_ids, counts):
    own, width = queries.shape
    shard = negatives.shape[0]
    parts = FAR * NEAR
    f32, f16 = jnp.float32, jnp.float16
    like = jax.ShapeDtypeStruct
    place = lax.axis_index("dp").astype(jnp.int32).reshape(1)
    spot = (lax.axis_index("neg").astype(jnp.int32) % NEAR).reshape(1)
    smem = pl.BlockSpec(memory_space=pltpu.SMEM)
    vmem = pl.BlockSpec(memory_space=pltpu.VMEM)
    hbm = pl.BlockSpec(memory_space=pltpu.HBM)
    rows = [[f * NEAR + n for n in range(NEAR)] for f in range(FAR)]
    sheets = [[g * CORES + c for g in range(LINE * RING)] for c in range(CORES)]

    across = mirror(queries)

    corr, score, ordered = pl.pallas_call(
        lookup_kernel,
        in_specs=[smem] + [vmem] * 6,
        out_specs=(vmem, vmem, vmem),
        out_shape=(
            like((shard // LANES, LANES), f32),
            like((1, own), f32),
            like((shard, width), jnp.bfloat16),
        ),
        scratch_shapes=[pltpu.VMEM((shard, LANES), f32)],
        compiler_params=params(),
        cost_estimate=cost(10**9, 2 * 10**6, 4096),
        name="lookup",
    )(
        place,
        counts.reshape(-1, LANES),
        neg_ids.reshape(-1, LANES),
        pos_ids.reshape(-1, LANES),
        queries,
        positives,
        negatives,
    )
    turned = ordered.T

    blocks = pl.pallas_call(
        spread_kernel,
        in_specs=[vmem] * 2,
        out_specs=vmem,
        out_shape=like((NEAR, FAR, own, width), jnp.bfloat16),
        compiler_params=params(),
        name="spread",
    )(queries, across)
    blocks = trade(blocks, "neg", rows)

    pairs = parts * own * shard
    fetched = [
        pltpu.VMEM((NEAR, FAR, own, width), jnp.bfloat16),
        pltpu.VMEM((shard, LANES), f32),
        pltpu.SemaphoreType.DMA,
    ]
    stats = pl.pallas_call(
        stats_kernel,
        in_specs=[smem, hbm] + [vmem] * 3,
        out_specs=vmem,
        out_shape=like((NEAR, parts, own), f32),
        scratch_shapes=fetched,
        compiler_params=params(),
        cost_estimate=cost(2 * pairs * width, 4 * 10**6, pairs),
        name="stats",
    )(spot, blocks, ordered, corr, score)
    joined = pl.pallas_call(
        join_kernel,
        in_specs=[vmem],
        out_specs=vmem,
        out_shape=like((parts, own), f32),
        compiler_params=params(),
        name="join",
    )(trade(stats, "neg", rows))
    other = mirror(joined)

    def grads(side, query_outs, *sums):
        neg_like = like((shard // CORES, width), f32)
        outs = [*query_outs, neg_like, neg_like, like((NEAR, own), f32)]
        return pl.pallas_call(
            functools.partial(grads_kernel, side),
            in_specs=[smem, hbm] + [vmem] * (5 + len(sums)),
            out_specs=(vmem,) * len(outs),
            out_shape=tuple(outs),
            scratch_shapes=[
                pltpu.VMEM((NEAR, own), f32),
                pltpu.VMEM((shard, NEAR * own), jnp.bfloat16),
                *fetched,
            ],
            compiler_params=params(32),
            cost_estimate=cost(3 * pairs * width, 8 * 10**6, pairs // 2),
            name="grads",
        )(spot, blocks, joined, other, ordered, turned, corr, *sums)

    far_terms, *sums, _ = grads(1, [like((NEAR, width, own), f32)])
    far_acc = trade(far_terms.astype(f16), "neg", rows).astype(f32).sum(axis=0)
    query_far = mirror(far_acc.astype(f16)).astype(f32)

    near_keep, near_send, keep, send, lse = grads(0, [like((2, width, own), f32)] * 2, *sums)
    from_core = other_core(send)
    got = swap_near(near_send.astype(f16), HALVING[0])
    onward = (near_keep[1] + got[1].astype(f32)).astype(f16)
    near_acc = near_keep[0] + got[0].astype(f32) + swap_near(onward, HALVING[1]).astype(f32)

    count = LINE * RING
    block = shard // CORES // count
    neg_acc = pl.pallas_call(
        sum_cores_kernel,
        in_specs=[vmem] * 2,
        out_specs=vmem,
        out_shape=like((count, block + 8, width), f32),
        compiler_params=params(),
        name="sum_cores",
    )(keep, from_core)
    neg_acc = trade(neg_acc.astype(f16), "dp", sheets).astype(f32)
    power = jnp.exp2(neg_acc[:, block : block + 1, :1] - 13.0)
    neg_grad = jnp.sum(neg_acc[:, :block, :] * power, axis=0)

    query_grad, row_loss = pl.pallas_call(
        finish_kernel,
        in_specs=[smem] + [vmem] * 7,
        out_specs=(vmem, vmem),
        out_shape=(like((own, width), f32), like((1, own), f32)),
        compiler_params=params(),
        name="finish",
    )(spot, near_acc, query_far, positives, score, lse, joined, other)
    return (query_grad, row_loss.reshape(own), neg_grad)


def solution(mesh):
    placed = (
        P(("dp", "neg"), None),
        P(("dp", "neg"), None),
        P("neg", None),
        P(("dp", "neg")),
        P("neg"),
        P(),
    )
    return jax.shard_map(
        per_device,
        mesh=mesh,
        in_specs=placed,
        out_specs=(P(("dp", "neg"), None), P(("dp", "neg")), P(("neg", "dp"), None)),
        check_vma=False,
    )
```

```python
import functools
import jax
import jax.numpy as jnp
from jax import lax
from jax.experimental import pallas as pl
from jax.experimental.pallas import tpu as pltpu
from jax.sharding import PartitionSpec as P

LANES = 128
CHUNK = 512
SPLIT = 256
SPAN = 60.0
MIB = 1024 * 1024
FAR, NEAR = 2, 4
HALVING = ((3, 1), (1, 3))
LINE, RING, CORES = 4, 8, 2


def dot(a, b, dims):
    return lax.dot_general(a, b, (dims, ((), ())), preferred_element_type=jnp.float32)


def params(mib=16):
    return pltpu.CompilerParams(vmem_limit_bytes=mib * MIB)


def cost(flops, nbytes, exps):
    return pl.CostEstimate(flops=flops, bytes_accessed=nbytes, transcendentals=exps)


def mirror(value):
    perm = []
    for l in range(LINE):
        for g in range(RING * CORES):
            for n in range(FAR * NEAR):
                to = ((LINE - 1 - l) * RING * CORES + g) * FAR * NEAR + (n + NEAR) % (FAR * NEAR)
                perm.append(((l * RING * CORES + g) * FAR * NEAR + n, to))
    return lax.ppermute(value, ("dp", "neg"), perm)


def swap_near(value, bits):
    perm = [(index, index ^ bits) for index in range(FAR * NEAR)]
    return lax.ppermute(value, "neg", perm)


def other_core(value):
    perm = [(index, index ^ 1) for index in range(LINE * RING * CORES)]
    return lax.ppermute(value, "dp", perm)


def lookup_kernel(
    place_ref, counts_ref, neg_ids_ref, pos_ids_ref, queries_ref, pos_ref, negatives_ref,
    corr_ref, score_ref, order_ref, tall_ref,
):
    counts = counts_ref[...].astype(jnp.float32)
    high = jnp.floor(counts * 0.125)
    digits = jnp.concatenate([high, counts - 8.0 * high], axis=1)
    table = digits.T.astype(jnp.bfloat16)
    table_rows = counts_ref.shape[0]
    total = negatives_ref.shape[0]
    block = total // (LINE * RING * CORES)
    place = place_ref[0]
    core = place & (CORES - 1)

    def corrections(ids):
        row = ids >> 7
        column = ids & (LANES - 1)
        width = ids.shape[1]
        spots = lax.broadcasted_iota(jnp.int32, (table_rows, width), 0)
        hot = jnp.where(spots == row, 1.0, 0.0).astype(jnp.bfloat16)
        found = dot(table, hot, ((1,), (0,)))
        value = 8.0 * found[:LANES] + found[LANES:]
        lanes = lax.broadcasted_iota(jnp.int32, (LANES, width), 0)
        picked = jnp.sum(jnp.where(lanes == column, value, 0.0), axis=0, keepdims=True)
        return jnp.log(picked)

    def target(index):
        l, r, c = index // (RING * CORES), (index // CORES) % RING, index % CORES
        away = (c - core) & (CORES - 1)
        return pl.ds(pl.multiple_of((away * LINE + l) * RING * block, block) + r * block, block)

    for k in range(neg_ids_ref.shape[0]):
        corr = corrections(neg_ids_ref[k : k + 1, :])
        tall = jnp.broadcast_to(corr, (LANES, LANES)).T
        for b in range(LANES // block):
            rows = target(k * (LANES // block) + b)
            tall_ref[rows, :] = tall[b * block : (b + 1) * block, :]
    for k in range(total // LANES):
        corr_ref[k : k + 1, :] = tall_ref[k * LANES : (k + 1) * LANES, :].T[:1, :]
    for k in range(total // block):
        order_ref[target(k), :] = negatives_ref[k * block : (k + 1) * block, :]
    products = queries_ref[...].astype(jnp.float32) * pos_ref[...].astype(jnp.float32)
    scores = jnp.sum(products.T, axis=0, keepdims=True)
    for k in range(pos_ids_ref.shape[0]):
        corr = corrections(pos_ids_ref[k : k + 1, :])
        lanes = slice(k * LANES, (k + 1) * LANES)
        score_ref[:, lanes] = scores[:, lanes] - corr


def wide(block, width):
    return jnp.concatenate([block] * (width // LANES), axis=1)


def row_stats(block, negatives_ref, corr_ref):
    rows = block.shape[0]
    top = None
    for start in range(0, negatives_ref.shape[0], CHUNK):
        part = slice(start, start + CHUNK)
        scores = dot(negatives_ref[part, :], block, ((1,), (1,)))
        scores = scores - wide(corr_ref[part, :], rows)
        tiles = scores.reshape(CHUNK // 8, 8, rows)
        best = jnp.max(tiles, axis=0)
        if top is None:
            top = best
            mass = jnp.sum(jnp.exp(tiles - top[None]), axis=0)
        else:
            new = jnp.maximum(top, best)
            mass = mass * jnp.exp(top - new) + jnp.sum(jnp.exp(tiles - new[None]), axis=0)
            top = new
    row_max = jnp.max(top, axis=0, keepdims=True)
    return row_max, jnp.sum(mass * jnp.exp(top - row_max), axis=0, keepdims=True)


def to_columns(rows_ref, out_ref):
    for k in range(rows_ref.shape[0]):
        tall = jnp.broadcast_to(rows_ref[k : k + 1, :], (LANES, LANES)).T
        out_ref[k * LANES : (k + 1) * LANES, :] = tall


def stats_kernel(
    spot_ref, blocks_hbm, negatives_ref, rows_ref, score_ref, out_ref, blocks_ref, corr_ref, sem
):
    fetch = pltpu.make_async_copy(blocks_hbm, blocks_ref, sem)
    fetch.start()
    to_columns(rows_ref, corr_ref)
    fetch.wait()
    score = score_ref[...]
    for side in range(FAR):
        for k in range(NEAR):
            row_max, row_sum = row_stats(blocks_ref[k, side], negatives_ref, corr_ref)
            if side == 0:
                own = spot_ref[0] == k
                joined = jnp.where(own, jnp.maximum(row_max, score), row_max)
                extra = jnp.exp(jnp.where(own, score, joined) - joined)
                row_sum = row_sum * jnp.exp(row_max - joined) + jnp.where(own, extra, 0.0)
                row_max = joined
            lse = row_max + jnp.log(row_sum)
            place = side * NEAR + k
            for c in range(NEAR):
                out_ref[c, place : place + 1, :] = lse


def join(parts):
    top = functools.reduce(jnp.maximum, parts)
    return top + jnp.log(sum(jnp.exp(part - top) for part in parts))


def join_kernel(parts_ref, out_ref):
    out_ref[...] = join([parts_ref[c] for c in range(NEAR)])


def grads_kernel(
    spot_ref, blocks_hbm, joined_ref, other_ref, negatives_ref, turned_ref, rows_ref, *refs
):
    query_outs, refs = refs[: 2 * FAR], refs[2 * FAR :]
    keep_out, send_out, lse_out, boost_ref, weight_ref, blocks_ref, corr_ref, sem = refs
    fetch = pltpu.make_async_copy(blocks_hbm, blocks_ref, sem)
    fetch.start()
    to_columns(rows_ref, corr_ref)
    total = negatives_ref.shape[0]
    spot = spot_ref[0]
    joined = joined_ref[...]
    other = jnp.concatenate([other_ref[NEAR:, :], other_ref[:NEAR, :]], axis=0)
    lse_all = join([joined, other])
    lse_out[...] = lse_all
    boost_ref[...] = jnp.exp(jnp.minimum(lse_all - joined, SPAN))
    half = total // CORES
    fetch.wait()
    for side in range(FAR):
        places = [spot ^ k for k in range(NEAR)]
        lse = [lse_out[pl.ds(side * NEAR + k, 1), :] for k in places]
        lse = jnp.concatenate(lse, axis=1)
        block = jnp.concatenate([blocks_ref[k, side] for k in places], axis=0)
        rows = block.shape[0]
        own = rows // NEAR
        for start in range(0, total, SPLIT):
            part = slice(start, start + SPLIT)
            scores = dot(negatives_ref[part, :], block, ((1,), (1,)))
            scores = scores - wide(corr_ref[part, :], rows)
            weight = jnp.exp(scores - lse).astype(jnp.bfloat16)
            weight_ref[part, :] = weight
            neg_term = dot(weight, block, ((1,), (0,)))
            which, place = start // half, slice(start % half, start % half + SPLIT)
            out = (keep_out, send_out)[which]
            if side > 0:
                neg_term = out[place, :] + neg_term
            out[place, :] = neg_term
        first, onward = HALVING[side]
        for index, k in enumerate(places):
            weight = weight_ref[:, index * own : (index + 1) * own]
            term = dot(turned_ref[...], weight, ((1,), (0,)))
            out = query_outs[side * 2 + (index in (first, first ^ onward))]
            place = int(index in (onward, first ^ onward))
            out[place] = term * boost_ref[pl.ds(side * NEAR + k, 1), :]


def spread_kernel(near_ref, far_ref, out_ref):
    for k in range(NEAR):
        out_ref[k, 0] = near_ref[...]
        out_ref[k, 1] = far_ref[...]


def sum_cores_kernel(keep_ref, got_ref, arrived_ref, out_ref):
    total = keep_ref[...] + got_ref[...]
    top = jnp.max(jnp.max(jnp.abs(total), axis=0, keepdims=True), axis=1, keepdims=True)
    power = jnp.clip(jnp.floor(jnp.log2(jnp.maximum(top, 1e-30))), -99.0, 99.0)
    scaled = total * jnp.exp2(13.0 - power)
    count, padded, width = out_ref.shape
    block = total.shape[0] // count
    for k in range(count):
        out_ref[k, :block, :] = scaled[k * block : (k + 1) * block, :]
        out_ref[k, block:, :] = jnp.broadcast_to(power, (padded - block, width))


def finish_kernel(
    spot_ref, near_ref, far_ref, pos_ref, score_ref, lse_ref, joined_ref, other_ref,
    grad_ref, loss_ref,
):
    spot = spot_ref[0]
    lse = lse_ref[pl.ds(spot, 1), :]
    near_share = jnp.exp(-jnp.minimum(lse - joined_ref[pl.ds(spot, 1), :], SPAN))
    far_share = jnp.exp(-jnp.minimum(lse - other_ref[pl.ds(spot + NEAR, 1), :], SPAN))
    score = score_ref[...]
    pos_weight = jnp.exp(score - lse)
    turned = near_ref[...] * near_share + far_ref[...] * far_share
    turned = turned + (pos_weight - 1.0) * pos_ref[...].astype(jnp.float32).T
    grad_ref[...] = turned.T
    loss_ref[...] = lse - score


def trade(value, axis, groups):
    return lax.all_to_all(value, axis, 0, 0, tiled=True, axis_index_groups=groups)


def per_device(queries, positives, negatives, pos_ids, neg_ids, counts):
    own, width = queries.shape
    shard = negatives.shape[0]
    parts = FAR * NEAR
    f32, f16 = jnp.float32, jnp.float16
    like = jax.ShapeDtypeStruct
    place = lax.axis_index("dp").astype(jnp.int32).reshape(1)
    spot = (lax.axis_index("neg").astype(jnp.int32) % NEAR).reshape(1)
    smem = pl.BlockSpec(memory_space=pltpu.SMEM)
    vmem = pl.BlockSpec(memory_space=pltpu.VMEM)
    hbm = pl.BlockSpec(memory_space=pltpu.HBM)
    rows = [[f * NEAR + n for n in range(NEAR)] for f in range(FAR)]
    sheets = [[g * CORES + c for g in range(LINE * RING)] for c in range(CORES)]

    across = mirror(queries)

    corr, score, ordered = pl.pallas_call(
        lookup_kernel,
        in_specs=[smem] + [vmem] * 6,
        out_specs=(vmem, vmem, vmem),
        out_shape=(
            like((shard // LANES, LANES), f32),
            like((1, own), f32),
            like((shard, width), jnp.bfloat16),
        ),
        scratch_shapes=[pltpu.VMEM((shard, LANES), f32)],
        compiler_params=params(),
        cost_estimate=cost(10**9, 2 * 10**6, 4096),
        name="lookup",
    )(
        place,
        counts.reshape(-1, LANES),
        neg_ids.reshape(-1, LANES),
        pos_ids.reshape(-1, LANES),
        queries,
        positives,
        negatives,
    )
    turned = ordered.T

    blocks = pl.pallas_call(
        spread_kernel,
        in_specs=[vmem] * 2,
        out_specs=vmem,
        out_shape=like((NEAR, FAR, own, width), jnp.bfloat16),
        compiler_params=params(),
        name="spread",
    )(queries, across)
    blocks = trade(blocks, "neg", rows)

    pairs = parts * own * shard
    fetched = [
        pltpu.VMEM((NEAR, FAR, own, width), jnp.bfloat16),
        pltpu.VMEM((shard, LANES), f32),
        pltpu.SemaphoreType.DMA,
    ]
    stats = pl.pallas_call(
        stats_kernel,
        in_specs=[smem, hbm] + [vmem] * 3,
        out_specs=vmem,
        out_shape=like((NEAR, parts, own), f32),
        scratch_shapes=fetched,
        compiler_params=params(),
        cost_estimate=cost(2 * pairs * width, 4 * 10**6, pairs),
        name="stats",
    )(spot, blocks, ordered, corr, score)
    joined = pl.pallas_call(
        join_kernel,
        in_specs=[vmem],
        out_specs=vmem,
        out_shape=like((parts, own), f32),
        compiler_params=params(),
        name="join",
    )(trade(stats, "neg", rows))
    other = mirror(joined)

    near_keep, near_send, far_keep, far_send, keep, send, lse = pl.pallas_call(
        grads_kernel,
        in_specs=[smem, hbm] + [vmem] * 5,
        out_specs=(vmem,) * (2 * FAR + 3),
        out_shape=(
            *[like((2, width, own), f32)] * (2 * FAR),
            like((shard // CORES, width), f32),
            like((shard // CORES, width), f32),
            like((parts, own), f32),
        ),
        scratch_shapes=[
            pltpu.VMEM((parts, own), f32),
            pltpu.VMEM((shard, NEAR * own), jnp.bfloat16),
            *fetched,
        ],
        compiler_params=params(24),
        cost_estimate=cost(6 * pairs * width, 8 * 10**6, pairs),
        name="grads",
    )(spot, blocks, joined, other, ordered, turned, corr)
    from_core = other_core(send)

    def halve(side, keep, got):
        sent = (keep[1] + got[1].astype(f32)).astype(f16)
        sent = swap_near(sent, HALVING[side][1])
        return keep[0] + got[0].astype(f32) + sent.astype(f32)

    far_got = swap_near(far_send.astype(f16), HALVING[1][0])
    near_got = swap_near(near_send.astype(f16), HALVING[0][0])
    arrived = near_got[0, :8, :LANES].astype(f32) + far_got[0, :8, :LANES].astype(f32)
    far_acc = halve(1, far_keep, far_got)
    near_acc = halve(0, near_keep, near_got)
    query_far = mirror(far_acc.astype(f16)).astype(f32)

    count = LINE * RING
    block = shard // CORES // count
    neg_acc = pl.pallas_call(
        sum_cores_kernel,
        in_specs=[vmem] * 3,
        out_specs=vmem,
        out_shape=like((count, block + 8, width), f32),
        compiler_params=params(),
        cost_estimate=cost(10**6, 10**6, 0),
        name="sum_cores",
    )(keep, from_core, arrived)
    neg_acc = trade(neg_acc.astype(f16), "dp", sheets).astype(f32)
    power = jnp.exp2(neg_acc[:, block : block + 1, :1] - 13.0)
    neg_grad = jnp.sum(neg_acc[:, :block, :] * power, axis=0)

    query_grad, row_loss = pl.pallas_call(
        finish_kernel,
        in_specs=[smem] + [vmem] * 7,
        out_specs=(vmem, vmem),
        out_shape=(like((own, width), f32), like((1, own), f32)),
        compiler_params=params(),
        name="finish",
    )(spot, near_acc, query_far, positives, score, lse, joined, other)
    return (query_grad, row_loss.reshape(own), neg_grad)


def solution(mesh):
    placed = (
        P(("dp", "neg"), None),
        P(("dp", "neg"), None),
        P("neg", None),
        P(("dp", "neg")),
        P("neg"),
        P(),
    )
    return jax.shard_map(
        per_device,
        mesh=mesh,
        in_specs=placed,
        out_specs=(P(("dp", "neg"), None), P(("dp", "neg")), P(("neg", "dp"), None)),
        check_vma=False,
    )
```

```python
import functools
import jax
import jax.numpy as jnp
from jax import lax
from jax.experimental import pallas as pl
from jax.experimental.pallas import tpu as pltpu
from jax.sharding import PartitionSpec as P

LANES = 128
CHUNK = 512
SPLIT = 256
SPAN = 60.0
MIB = 1024 * 1024
FAR, NEAR = 2, 4
HALVING = ((3, 1), (1, 3))
LINE, RING, CORES = 4, 8, 2


def dot(a, b, dims):
    return lax.dot_general(a, b, (dims, ((), ())), preferred_element_type=jnp.float32)


def params(mib=16):
    return pltpu.CompilerParams(vmem_limit_bytes=mib * MIB)


def cost(flops, nbytes, exps):
    return pl.CostEstimate(flops=flops, bytes_accessed=nbytes, transcendentals=exps)


def mirror(value):
    perm = []
    for l in range(LINE):
        for g in range(RING * CORES):
            for n in range(FAR * NEAR):
                to = ((LINE - 1 - l) * RING * CORES + g) * FAR * NEAR + (n + NEAR) % (FAR * NEAR)
                perm.append(((l * RING * CORES + g) * FAR * NEAR + n, to))
    return lax.ppermute(value, ("dp", "neg"), perm)


def swap_near(value, bits):
    perm = [(index, index ^ bits) for index in range(FAR * NEAR)]
    return lax.ppermute(value, "neg", perm)


def other_core(value):
    perm = [(index, index ^ 1) for index in range(LINE * RING * CORES)]
    return lax.ppermute(value, "dp", perm)


def lookup_kernel(
    place_ref, counts_ref, neg_ids_ref, pos_ids_ref, queries_ref, pos_ref, negatives_ref,
    corr_ref, score_ref, order_ref, tall_ref,
):
    counts = counts_ref[...].astype(jnp.float32)
    high = jnp.floor(counts * 0.125)
    digits = jnp.concatenate([high, counts - 8.0 * high], axis=1)
    table = digits.T.astype(jnp.bfloat16)
    table_rows = counts_ref.shape[0]
    total = negatives_ref.shape[0]
    block = total // (LINE * RING * CORES)
    place = place_ref[0]
    core = place & (CORES - 1)

    def corrections(ids):
        row = ids >> 7
        column = ids & (LANES - 1)
        width = ids.shape[1]
        spots = lax.broadcasted_iota(jnp.int32, (table_rows, width), 0)
        hot = jnp.where(spots == row, 1.0, 0.0).astype(jnp.bfloat16)
        found = dot(table, hot, ((1,), (0,)))
        value = 8.0 * found[:LANES] + found[LANES:]
        lanes = lax.broadcasted_iota(jnp.int32, (LANES, width), 0)
        picked = jnp.sum(jnp.where(lanes == column, value, 0.0), axis=0, keepdims=True)
        return jnp.log(picked)

    def target(index):
        l, r, c = index // (RING * CORES), (index // CORES) % RING, index % CORES
        away = (c - core) & (CORES - 1)
        return pl.ds(pl.multiple_of((away * LINE + l) * RING * block, block) + r * block, block)

    for k in range(neg_ids_ref.shape[0]):
        corr = corrections(neg_ids_ref[k : k + 1, :])
        tall = jnp.broadcast_to(corr, (LANES, LANES)).T
        for b in range(LANES // block):
            rows = target(k * (LANES // block) + b)
            tall_ref[rows, :] = tall[b * block : (b + 1) * block, :]
    for k in range(total // LANES):
        corr_ref[k : k + 1, :] = tall_ref[k * LANES : (k + 1) * LANES, :].T[:1, :]
    for k in range(total // block):
        order_ref[target(k), :] = negatives_ref[k * block : (k + 1) * block, :]
    products = queries_ref[...].astype(jnp.float32) * pos_ref[...].astype(jnp.float32)
    scores = jnp.sum(products.T, axis=0, keepdims=True)
    for k in range(pos_ids_ref.shape[0]):
        corr = corrections(pos_ids_ref[k : k + 1, :])
        lanes = slice(k * LANES, (k + 1) * LANES)
        score_ref[:, lanes] = scores[:, lanes] - corr


def wide(block, width):
    return jnp.concatenate([block] * (width // LANES), axis=1)


def row_stats(block, negatives_ref, corr_ref):
    rows = block.shape[0]
    top = None
    for start in range(0, negatives_ref.shape[0], CHUNK):
        part = slice(start, start + CHUNK)
        scores = dot(negatives_ref[part, :], block, ((1,), (1,)))
        scores = scores - wide(corr_ref[part, :], rows)
        tiles = scores.reshape(CHUNK // 8, 8, rows)
        best = jnp.max(tiles, axis=0)
        if top is None:
            top = best
            mass = jnp.sum(jnp.exp(tiles - top[None]), axis=0)
        else:
            new = jnp.maximum(top, best)
            mass = mass * jnp.exp(top - new) + jnp.sum(jnp.exp(tiles - new[None]), axis=0)
            top = new
    row_max = jnp.max(top, axis=0, keepdims=True)
    return row_max, jnp.sum(mass * jnp.exp(top - row_max), axis=0, keepdims=True)


def to_columns(rows_ref, out_ref):
    for k in range(rows_ref.shape[0]):
        tall = jnp.broadcast_to(rows_ref[k : k + 1, :], (LANES, LANES)).T
        out_ref[k * LANES : (k + 1) * LANES, :] = tall


def near_stats_kernel(
    spot_ref, own_ref, first_ref, second_ref, negatives_ref, rows_ref, score_ref, out_ref, corr_ref
):
    to_columns(rows_ref, corr_ref)
    for k, block in enumerate(near_order(own_ref, first_ref, second_ref)):
        row_max, row_sum = row_stats(block, negatives_ref, corr_ref)
        if k == 0:
            score = score_ref[...]
            joined = jnp.maximum(row_max, score)
            row_sum = row_sum * jnp.exp(row_max - joined) + jnp.exp(score - joined)
            row_max = joined
        out_ref[pl.ds(spot_ref[0] ^ k, 1), :] = row_max + jnp.log(row_sum)


def far_stats_kernel(
    blocks_hbm, negatives_ref, rows_ref, near_ref, out_ref, blocks_ref, corr_ref, sem
):
    fetch = pltpu.make_async_copy(blocks_hbm, blocks_ref, sem)
    fetch.start()
    to_columns(rows_ref, corr_ref)
    for c in range(NEAR):
        out_ref[c, :NEAR, :] = near_ref[...]
    fetch.wait()
    for k in range(NEAR):
        row_max, row_sum = row_stats(blocks_ref[k], negatives_ref, corr_ref)
        lse = row_max + jnp.log(row_sum)
        for c in range(NEAR):
            out_ref[c, NEAR + k : NEAR + k + 1, :] = lse


def near_order(own_ref, first_ref, second_ref):
    return [own_ref[...], second_ref[0], second_ref[1], first_ref[...]]


def join(parts):
    top = functools.reduce(jnp.maximum, parts)
    return top + jnp.log(sum(jnp.exp(part - top) for part in parts))


def join_kernel(parts_ref, out_ref):
    out_ref[...] = join([parts_ref[c] for c in range(NEAR)])


def grads_kernel(
    spot_ref, own_ref, first_ref, second_ref, blocks_hbm, joined_ref, other_ref, negatives_ref,
    turned_ref, rows_ref, *refs
):
    query_outs, refs = refs[: 2 * FAR], refs[2 * FAR :]
    keep_out, send_out, lse_out, boost_ref, weight_ref, blocks_ref, corr_ref, sem = refs
    fetch = pltpu.make_async_copy(blocks_hbm, blocks_ref, sem)
    fetch.start()
    to_columns(rows_ref, corr_ref)
    total = negatives_ref.shape[0]
    spot = spot_ref[0]
    joined = joined_ref[...]
    other = jnp.concatenate([other_ref[NEAR:, :], other_ref[:NEAR, :]], axis=0)
    lse_all = join([joined, other])
    lse_out[...] = lse_all
    boost_ref[...] = jnp.exp(jnp.minimum(lse_all - joined, SPAN))
    half = total // CORES
    for side in range(FAR):
        places = [spot ^ k for k in range(NEAR)]
        lse = [lse_out[pl.ds(side * NEAR + k, 1), :] for k in places]
        lse = jnp.concatenate(lse, axis=1)
        if side == 0:
            block = near_order(own_ref, first_ref, second_ref)
        else:
            fetch.wait()
            block = [blocks_ref[k] for k in places]
        block = jnp.concatenate(block, axis=0)
        rows = block.shape[0]
        own = rows // NEAR
        for start in range(0, total, SPLIT):
            part = slice(start, start + SPLIT)
            scores = dot(negatives_ref[part, :], block, ((1,), (1,)))
            scores = scores - wide(corr_ref[part, :], rows)
            weight = jnp.exp(scores - lse).astype(jnp.bfloat16)
            weight_ref[part, :] = weight
            neg_term = dot(weight, block, ((1,), (0,)))
            which, place = start // half, slice(start % half, start % half + SPLIT)
            out = (keep_out, send_out)[which]
            if side > 0:
                neg_term = out[place, :] + neg_term
            out[place, :] = neg_term
        first, onward = HALVING[side]
        for index, k in enumerate(places):
            weight = weight_ref[:, index * own : (index + 1) * own]
            term = dot(turned_ref[...], weight, ((1,), (0,)))
            out = query_outs[side * 2 + (index in (first, first ^ onward))]
            place = int(index in (onward, first ^ onward))
            out[place] = term * boost_ref[pl.ds(side * NEAR + k, 1), :]


def spread_kernel(block_ref, arrived_ref, out_ref):
    for k in range(NEAR):
        out_ref[k] = block_ref[...]


def sum_cores_kernel(keep_ref, got_ref, arrived_ref, out_ref):
    total = keep_ref[...] + got_ref[...]
    top = jnp.max(jnp.max(jnp.abs(total), axis=0, keepdims=True), axis=1, keepdims=True)
    power = jnp.clip(jnp.floor(jnp.log2(jnp.maximum(top, 1e-30))), -99.0, 99.0)
    scaled = total * jnp.exp2(13.0 - power)
    count, padded, width = out_ref.shape
    block = total.shape[0] // count
    for k in range(count):
        out_ref[k, :block, :] = scaled[k * block : (k + 1) * block, :]
        out_ref[k, block:, :] = jnp.broadcast_to(power, (padded - block, width))


def finish_kernel(
    spot_ref, near_ref, far_ref, pos_ref, score_ref, lse_ref, joined_ref, other_ref,
    grad_ref, loss_ref,
):
    spot = spot_ref[0]
    lse = lse_ref[pl.ds(spot, 1), :]
    near_share = jnp.exp(-jnp.minimum(lse - joined_ref[pl.ds(spot, 1), :], SPAN))
    far_share = jnp.exp(-jnp.minimum(lse - other_ref[pl.ds(spot + NEAR, 1), :], SPAN))
    score = score_ref[...]
    pos_weight = jnp.exp(score - lse)
    turned = near_ref[...] * near_share + far_ref[...] * far_share
    turned = turned + (pos_weight - 1.0) * pos_ref[...].astype(jnp.float32).T
    grad_ref[...] = turned.T
    loss_ref[...] = lse - score


def trade(value, axis, groups):
    return lax.all_to_all(value, axis, 0, 0, tiled=True, axis_index_groups=groups)


def per_device(queries, positives, negatives, pos_ids, neg_ids, counts):
    own, width = queries.shape
    shard = negatives.shape[0]
    parts = FAR * NEAR
    f32, f16 = jnp.float32, jnp.float16
    like = jax.ShapeDtypeStruct
    place = lax.axis_index("dp").astype(jnp.int32).reshape(1)
    spot = (lax.axis_index("neg").astype(jnp.int32) % NEAR).reshape(1)
    smem = pl.BlockSpec(memory_space=pltpu.SMEM)
    vmem = pl.BlockSpec(memory_space=pltpu.VMEM)
    hbm = pl.BlockSpec(memory_space=pltpu.HBM)
    rows = [[f * NEAR + n for n in range(NEAR)] for f in range(FAR)]
    sheets = [[g * CORES + c for g in range(LINE * RING)] for c in range(CORES)]

    across = mirror(queries)
    first = swap_near(queries, 3)

    corr, score, ordered = pl.pallas_call(
        lookup_kernel,
        in_specs=[smem] + [vmem] * 6,
        out_specs=(vmem, vmem, vmem),
        out_shape=(
            like((shard // LANES, LANES), f32),
            like((1, own), f32),
            like((shard, width), jnp.bfloat16),
        ),
        scratch_shapes=[pltpu.VMEM((shard, LANES), f32)],
        compiler_params=params(),
        cost_estimate=cost(10**9, 2 * 10**6, 4096),
        name="lookup",
    )(
        place,
        counts.reshape(-1, LANES),
        neg_ids.reshape(-1, LANES),
        pos_ids.reshape(-1, LANES),
        queries,
        positives,
        negatives,
    )
    turned = ordered.T

    far_blocks = pl.pallas_call(
        spread_kernel,
        in_specs=[vmem, hbm],
        out_specs=vmem,
        out_shape=like((NEAR, own, width), jnp.bfloat16),
        compiler_params=params(),
        cost_estimate=cost(10**6, 10**6, 0),
        name="spread",
    )(across, first)
    far_blocks = trade(far_blocks, "neg", rows)
    near_blocks = (queries, first, swap_near(jnp.stack([queries, first]), 1))

    pairs = parts * own * shard
    fetched = [
        pltpu.VMEM((NEAR, own, width), jnp.bfloat16),
        pltpu.VMEM((shard, LANES), f32),
        pltpu.SemaphoreType.DMA,
    ]
    near_stats = pl.pallas_call(
        near_stats_kernel,
        in_specs=[smem] + [vmem] * 6,
        out_specs=vmem,
        out_shape=like((NEAR, own), f32),
        scratch_shapes=[pltpu.VMEM((shard, LANES), f32)],
        compiler_params=params(),
        cost_estimate=cost(pairs * width, 2 * 10**6, pairs // 2),
        name="near_stats",
    )(spot, *near_blocks, ordered, corr, score)
    stats = pl.pallas_call(
        far_stats_kernel,
        in_specs=[hbm] + [vmem] * 3,
        out_specs=vmem,
        out_shape=like((NEAR, parts, own), f32),
        scratch_shapes=fetched,
        compiler_params=params(),
        cost_estimate=cost(pairs * width, 2 * 10**6, pairs // 2),
        name="far_stats",
    )(far_blocks, ordered, corr, near_stats)
    joined = pl.pallas_call(
        join_kernel,
        in_specs=[vmem],
        out_specs=vmem,
        out_shape=like((parts, own), f32),
        compiler_params=params(),
        name="join",
    )(trade(stats, "neg", rows))
    other = mirror(joined)

    near_keep, near_send, far_keep, far_send, keep, send, lse = pl.pallas_call(
        grads_kernel,
        in_specs=[smem] + [vmem] * 3 + [hbm] + [vmem] * 5,
        out_specs=(vmem,) * (2 * FAR + 3),
        out_shape=(
            *[like((2, width, own), f32)] * (2 * FAR),
            like((shard // CORES, width), f32),
            like((shard // CORES, width), f32),
            like((parts, own), f32),
        ),
        scratch_shapes=[
            pltpu.VMEM((parts, own), f32),
            pltpu.VMEM((shard, NEAR * own), jnp.bfloat16),
            *fetched,
        ],
        compiler_params=params(24),
        cost_estimate=cost(6 * pairs * width, 8 * 10**6, pairs),
        name="grads",
    )(spot, *near_blocks, far_blocks, joined, other, ordered, turned, corr)
    from_core = other_core(send)

    def halve(side, keep, got):
        sent = (keep[1] + got[1].astype(f32)).astype(f16)
        sent = swap_near(sent, HALVING[side][1])
        return keep[0] + got[0].astype(f32) + sent.astype(f32)

    far_got = swap_near(far_send.astype(f16), HALVING[1][0])
    near_got = swap_near(near_send.astype(f16), HALVING[0][0])
    arrived = near_got[0, :8, :LANES].astype(f32) + far_got[0, :8, :LANES].astype(f32)
    far_acc = halve(1, far_keep, far_got)
    near_acc = halve(0, near_keep, near_got)
    query_far = mirror(far_acc.astype(f16)).astype(f32)

    count = LINE * RING
    block = shard // CORES // count
    neg_acc = pl.pallas_call(
        sum_cores_kernel,
        in_specs=[vmem] * 3,
        out_specs=vmem,
        out_shape=like((count, block + 8, width), f32),
        compiler_params=params(),
        cost_estimate=cost(10**6, 10**6, 0),
        name="sum_cores",
    )(keep, from_core, arrived)
    neg_acc = trade(neg_acc.astype(f16), "dp", sheets).astype(f32)
    power = jnp.exp2(neg_acc[:, block : block + 1, :1] - 13.0)
    neg_grad = jnp.sum(neg_acc[:, :block, :] * power, axis=0)

    query_grad, row_loss = pl.pallas_call(
        finish_kernel,
        in_specs=[smem] + [vmem] * 7,
        out_specs=(vmem, vmem),
        out_shape=(like((own, width), f32), like((1, own), f32)),
        compiler_params=params(),
        name="finish",
    )(spot, near_acc, query_far, positives, score, lse, joined, other)
    return (query_grad, row_loss.reshape(own), neg_grad)


def solution(mesh):
    placed = (
        P(("dp", "neg"), None),
        P(("dp", "neg"), None),
        P("neg", None),
        P(("dp", "neg")),
        P("neg"),
        P(),
    )
    return jax.shard_map(
        per_device,
        mesh=mesh,
        in_specs=placed,
        out_specs=(P(("dp", "neg"), None), P(("dp", "neg")), P(("neg", "dp"), None)),
        check_vma=False,
    )
```

```python
import functools
import jax
import jax.numpy as jnp
from jax import lax
from jax.experimental import pallas as pl
from jax.experimental.pallas import tpu as pltpu
from jax.sharding import PartitionSpec as P

LANES = 128
CHUNK = 512
SPLIT = 256
SPAN = 60.0
MIB = 1024 * 1024
FAR, NEAR = 2, 4
HALVING = ((3, 1), (1, 3))
LINE, RING, CORES = 4, 8, 2


def dot(a, b, dims):
    return lax.dot_general(a, b, (dims, ((), ())), preferred_element_type=jnp.float32)


def params(mib=16):
    return pltpu.CompilerParams(vmem_limit_bytes=mib * MIB)


def cost(flops, nbytes, exps):
    return pl.CostEstimate(flops=flops, bytes_accessed=nbytes, transcendentals=exps)


def mirror(value):
    perm = []
    for l in range(LINE):
        for g in range(RING * CORES):
            for n in range(FAR * NEAR):
                to = ((LINE - 1 - l) * RING * CORES + g) * FAR * NEAR + (n + NEAR) % (FAR * NEAR)
                perm.append(((l * RING * CORES + g) * FAR * NEAR + n, to))
    return lax.ppermute(value, ("dp", "neg"), perm)


def swap_near(value, bits):
    perm = [(index, index ^ bits) for index in range(FAR * NEAR)]
    return lax.ppermute(value, "neg", perm)


def other_core(value):
    perm = [(index, index ^ 1) for index in range(LINE * RING * CORES)]
    return lax.ppermute(value, "dp", perm)


def lookup_kernel(
    place_ref, counts_ref, neg_ids_ref, pos_ids_ref, queries_ref, pos_ref, negatives_ref,
    corr_ref, score_ref, order_ref, tall_ref,
):
    counts = counts_ref[...].astype(jnp.float32)
    high = jnp.floor(counts * 0.125)
    digits = jnp.concatenate([high, counts - 8.0 * high], axis=1)
    table = digits.T.astype(jnp.bfloat16)
    table_rows = counts_ref.shape[0]
    total = negatives_ref.shape[0]
    block = total // (LINE * RING * CORES)
    place = place_ref[0]
    core = place & (CORES - 1)

    def corrections(ids):
        row = ids >> 7
        column = ids & (LANES - 1)
        width = ids.shape[1]
        spots = lax.broadcasted_iota(jnp.int32, (table_rows, width), 0)
        hot = jnp.where(spots == row, 1.0, 0.0).astype(jnp.bfloat16)
        found = dot(table, hot, ((1,), (0,)))
        value = 8.0 * found[:LANES] + found[LANES:]
        lanes = lax.broadcasted_iota(jnp.int32, (LANES, width), 0)
        picked = jnp.sum(jnp.where(lanes == column, value, 0.0), axis=0, keepdims=True)
        return jnp.log(picked)

    def target(index):
        l, r, c = index // (RING * CORES), (index // CORES) % RING, index % CORES
        away = (c - core) & (CORES - 1)
        return pl.ds(pl.multiple_of((away * LINE + l) * RING * block, block) + r * block, block)

    for k in range(neg_ids_ref.shape[0]):
        corr = corrections(neg_ids_ref[k : k + 1, :])
        tall = jnp.broadcast_to(corr, (LANES, LANES)).T
        for b in range(LANES // block):
            rows = target(k * (LANES // block) + b)
            tall_ref[rows, :] = tall[b * block : (b + 1) * block, :]
    for k in range(total // LANES):
        corr_ref[k : k + 1, :] = tall_ref[k * LANES : (k + 1) * LANES, :].T[:1, :]
    for k in range(total // block):
        order_ref[target(k), :] = negatives_ref[k * block : (k + 1) * block, :]
    products = queries_ref[...].astype(jnp.float32) * pos_ref[...].astype(jnp.float32)
    scores = jnp.sum(products.T, axis=0, keepdims=True)
    for k in range(pos_ids_ref.shape[0]):
        corr = corrections(pos_ids_ref[k : k + 1, :])
        lanes = slice(k * LANES, (k + 1) * LANES)
        score_ref[:, lanes] = scores[:, lanes] - corr


def wide(block, width):
    return jnp.concatenate([block] * (width // LANES), axis=1)


def row_stats(block, negatives_ref, corr_ref):
    rows = block.shape[0]
    top = None
    for start in range(0, negatives_ref.shape[0], CHUNK):
        part = slice(start, start + CHUNK)
        scores = dot(negatives_ref[part, :], block, ((1,), (1,)))
        scores = scores - wide(corr_ref[part, :], rows)
        tiles = scores.reshape(CHUNK // 8, 8, rows)
        best = jnp.max(tiles, axis=0)
        if top is None:
            top = best
            mass = jnp.sum(jnp.exp(tiles - top[None]), axis=0)
        else:
            new = jnp.maximum(top, best)
            mass = mass * jnp.exp(top - new) + jnp.sum(jnp.exp(tiles - new[None]), axis=0)
            top = new
    row_max = jnp.max(top, axis=0, keepdims=True)
    return row_max, jnp.sum(mass * jnp.exp(top - row_max), axis=0, keepdims=True)


def to_columns(rows_ref, out_ref):
    for k in range(rows_ref.shape[0]):
        tall = jnp.broadcast_to(rows_ref[k : k + 1, :], (LANES, LANES)).T
        out_ref[k * LANES : (k + 1) * LANES, :] = tall


def stats_kernel(
    spot_ref, blocks_hbm, negatives_ref, rows_ref, score_ref, out_ref, blocks_ref, corr_ref, sem
):
    fetch = pltpu.make_async_copy(blocks_hbm, blocks_ref, sem)
    fetch.start()
    to_columns(rows_ref, corr_ref)
    fetch.wait()
    score = score_ref[...]
    for side in range(FAR):
        for k in range(NEAR):
            row_max, row_sum = row_stats(blocks_ref[k, side], negatives_ref, corr_ref)
            if side == 0:
                own = spot_ref[0] == k
                joined = jnp.where(own, jnp.maximum(row_max, score), row_max)
                extra = jnp.exp(jnp.where(own, score, joined) - joined)
                row_sum = row_sum * jnp.exp(row_max - joined) + jnp.where(own, extra, 0.0)
                row_max = joined
            lse = row_max + jnp.log(row_sum)
            place = side * NEAR + k
            for c in range(NEAR):
                out_ref[c, place : place + 1, :] = lse


def join(parts):
    top = functools.reduce(jnp.maximum, parts)
    return top + jnp.log(sum(jnp.exp(part - top) for part in parts))


def join_kernel(parts_ref, out_ref):
    out_ref[...] = join([parts_ref[c] for c in range(NEAR)])


def grads_kernel(
    spot_ref, blocks_hbm, joined_ref, other_ref, negatives_ref, turned_ref, rows_ref, *refs
):
    query_outs, refs = refs[: 2 * FAR], refs[2 * FAR :]
    keep_out, send_out, lse_out, boost_ref, weight_ref, blocks_ref, corr_ref, sem = refs
    fetch = pltpu.make_async_copy(blocks_hbm, blocks_ref, sem)
    fetch.start()
    to_columns(rows_ref, corr_ref)
    total = negatives_ref.shape[0]
    spot = spot_ref[0]
    joined = joined_ref[...]
    other = jnp.concatenate([other_ref[NEAR:, :], other_ref[:NEAR, :]], axis=0)
    lse_all = join([joined, other])
    lse_out[...] = lse_all
    boost_ref[...] = jnp.exp(jnp.minimum(lse_all - joined, SPAN))
    half = total // CORES
    fetch.wait()
    for side in range(FAR):
        places = [spot ^ k for k in range(NEAR)]
        lse = [lse_out[pl.ds(side * NEAR + k, 1), :] for k in places]
        lse = jnp.concatenate(lse, axis=1)
        block = jnp.concatenate([blocks_ref[k, side] for k in places], axis=0)
        rows = block.shape[0]
        own = rows // NEAR
        for start in range(0, total, SPLIT):
            part = slice(start, start + SPLIT)
            scores = dot(negatives_ref[part, :], block, ((1,), (1,)))
            scores = scores - wide(corr_ref[part, :], rows)
            weight = jnp.exp(scores - lse).astype(jnp.bfloat16)
            weight_ref[part, :] = weight
            neg_term = dot(weight, block, ((1,), (0,)))
            which, place = start // half, slice(start % half, start % half + SPLIT)
            out = (keep_out, send_out)[which]
            if side > 0:
                neg_term = out[place, :] + neg_term
            out[place, :] = neg_term
        first, onward = HALVING[side]
        for index, k in enumerate(places):
            weight = weight_ref[:, index * own : (index + 1) * own]
            term = dot(turned_ref[...], weight, ((1,), (0,)))
            out = query_outs[side * 2 + (index in (first, first ^ onward))]
            place = int(index in (onward, first ^ onward))
            out[place] = term * boost_ref[pl.ds(side * NEAR + k, 1), :]


def spread_kernel(near_ref, far_ref, out_ref):
    for k in range(NEAR):
        out_ref[k, 0] = near_ref[...]
        out_ref[k, 1] = far_ref[...]


def halve_kernel(near_keep_ref, near_got_ref, far_keep_ref, far_got_ref, mine_ref, onward_ref):
    for side, (keep, got) in enumerate(
        ((near_keep_ref, near_got_ref), (far_keep_ref, far_got_ref))
    ):
        mine_ref[side] = keep[0] + got[0]
        onward_ref[side] = keep[1] + got[1]


def sum_cores_kernel(keep_ref, got_ref, out_ref):
    total = keep_ref[...] + got_ref[...]
    top = jnp.max(jnp.max(jnp.abs(total), axis=0, keepdims=True), axis=1, keepdims=True)
    power = jnp.clip(jnp.floor(jnp.log2(jnp.maximum(top, 1e-30))), -99.0, 99.0)
    scaled = total * jnp.exp2(13.0 - power)
    count, padded, width = out_ref.shape
    block = total.shape[0] // count
    for k in range(count):
        out_ref[k, :block, :] = scaled[k * block : (k + 1) * block, :]
        out_ref[k, block:, :] = jnp.broadcast_to(power, (padded - block, width))


def finish_kernel(
    spot_ref, near_ref, far_ref, pos_ref, score_ref, lse_ref, joined_ref, other_ref,
    grad_ref, loss_ref,
):
    spot = spot_ref[0]
    lse = lse_ref[pl.ds(spot, 1), :]
    near_share = jnp.exp(-jnp.minimum(lse - joined_ref[pl.ds(spot, 1), :], SPAN))
    far_share = jnp.exp(-jnp.minimum(lse - other_ref[pl.ds(spot + NEAR, 1), :], SPAN))
    score = score_ref[...]
    pos_weight = jnp.exp(score - lse)
    turned = near_ref[...] * near_share + far_ref[...] * far_share
    turned = turned + (pos_weight - 1.0) * pos_ref[...].astype(jnp.float32).T
    grad_ref[...] = turned.T
    loss_ref[...] = lse - score


def trade(value, axis, groups):
    return lax.all_to_all(value, axis, 0, 0, tiled=True, axis_index_groups=groups)


def per_device(queries, positives, negatives, pos_ids, neg_ids, counts):
    own, width = queries.shape
    shard = negatives.shape[0]
    parts = FAR * NEAR
    f32, f16 = jnp.float32, jnp.float16
    like = jax.ShapeDtypeStruct
    place = lax.axis_index("dp").astype(jnp.int32).reshape(1)
    spot = (lax.axis_index("neg").astype(jnp.int32) % NEAR).reshape(1)
    smem = pl.BlockSpec(memory_space=pltpu.SMEM)
    vmem = pl.BlockSpec(memory_space=pltpu.VMEM)
    hbm = pl.BlockSpec(memory_space=pltpu.HBM)
    rows = [[f * NEAR + n for n in range(NEAR)] for f in range(FAR)]
    sheets = [[g * CORES + c for g in range(LINE * RING)] for c in range(CORES)]

    across = mirror(queries)

    corr, score, ordered = pl.pallas_call(
        lookup_kernel,
        in_specs=[smem] + [vmem] * 6,
        out_specs=(vmem, vmem, vmem),
        out_shape=(
            like((shard // LANES, LANES), f32),
            like((1, own), f32),
            like((shard, width), jnp.bfloat16),
        ),
        scratch_shapes=[pltpu.VMEM((shard, LANES), f32)],
        compiler_params=params(),
        cost_estimate=cost(10**9, 2 * 10**6, 4096),
        name="lookup",
    )(
        place,
        counts.reshape(-1, LANES),
        neg_ids.reshape(-1, LANES),
        pos_ids.reshape(-1, LANES),
        queries,
        positives,
        negatives,
    )
    turned = ordered.T

    blocks = pl.pallas_call(
        spread_kernel,
        in_specs=[vmem] * 2,
        out_specs=vmem,
        out_shape=like((NEAR, FAR, own, width), jnp.bfloat16),
        compiler_params=params(),
        name="spread",
    )(queries, across)
    blocks = trade(blocks, "neg", rows)

    pairs = parts * own * shard
    fetched = [
        pltpu.VMEM((NEAR, FAR, own, width), jnp.bfloat16),
        pltpu.VMEM((shard, LANES), f32),
        pltpu.SemaphoreType.DMA,
    ]
    stats = pl.pallas_call(
        stats_kernel,
        in_specs=[smem, hbm] + [vmem] * 3,
        out_specs=vmem,
        out_shape=like((NEAR, parts, own), f32),
        scratch_shapes=fetched,
        compiler_params=params(),
        cost_estimate=cost(2 * pairs * width, 4 * 10**6, pairs),
        name="stats",
    )(spot, blocks, ordered, corr, score)
    joined = pl.pallas_call(
        join_kernel,
        in_specs=[vmem],
        out_specs=vmem,
        out_shape=like((parts, own), f32),
        compiler_params=params(),
        name="join",
    )(trade(stats, "neg", rows))
    other = mirror(joined)

    near_keep, near_send, far_keep, far_send, keep, send, lse = pl.pallas_call(
        grads_kernel,
        in_specs=[smem, hbm] + [vmem] * 5,
        out_specs=(vmem,) * (2 * FAR + 3),
        out_shape=(
            *[like((2, width, own), f32)] * (2 * FAR),
            like((shard // CORES, width), f32),
            like((shard // CORES, width), f32),
            like((parts, own), f32),
        ),
        scratch_shapes=[
            pltpu.VMEM((parts, own), f32),
            pltpu.VMEM((shard, NEAR * own), jnp.bfloat16),
            *fetched,
        ],
        compiler_params=params(24),
        cost_estimate=cost(6 * pairs * width, 8 * 10**6, pairs),
        name="grads",
    )(spot, blocks, joined, other, ordered, turned, corr)
    from_core = other_core(send)

    far_got = swap_near(far_send.astype(f16), HALVING[1][0]).astype(f32)
    near_got = swap_near(near_send.astype(f16), HALVING[0][0]).astype(f32)
    mine, onward = pl.pallas_call(
        halve_kernel,
        in_specs=[vmem] * 4,
        out_specs=(vmem,) * 2,
        out_shape=(like((FAR, width, own), f32),) * 2,
        compiler_params=params(),
        cost_estimate=cost(10**6, 2 * 10**8, 0),
        name="halve",
    )(near_keep, near_got, far_keep, far_got)
    far_acc = mine[1] + swap_near(onward[1].astype(f16), HALVING[1][1]).astype(f32)
    near_acc = mine[0] + swap_near(onward[0].astype(f16), HALVING[0][1]).astype(f32)
    query_far = mirror(far_acc.astype(f16)).astype(f32)

    count = LINE * RING
    block = shard // CORES // count
    neg_acc = pl.pallas_call(
        sum_cores_kernel,
        in_specs=[vmem] * 2,
        out_specs=vmem,
        out_shape=like((count, block + 8, width), f32),
        compiler_params=params(),
        cost_estimate=cost(10**6, 10**6, 0),
        name="sum_cores",
    )(keep, from_core)
    neg_acc = trade(neg_acc.astype(f16), "dp", sheets).astype(f32)
    power = jnp.exp2(neg_acc[:, block : block + 1, :1] - 13.0)
    neg_grad = jnp.sum(neg_acc[:, :block, :] * power, axis=0)

    query_grad, row_loss = pl.pallas_call(
        finish_kernel,
        in_specs=[smem] + [vmem] * 7,
        out_specs=(vmem, vmem),
        out_shape=(like((own, width), f32), like((1, own), f32)),
        compiler_params=params(),
        name="finish",
    )(spot, near_acc, query_far, positives, score, lse, joined, other)
    return (query_grad, row_loss.reshape(own), neg_grad)


def solution(mesh):
    placed = (
        P(("dp", "neg"), None),
        P(("dp", "neg"), None),
        P("neg", None),
        P(("dp", "neg")),
        P("neg"),
        P(),
    )
    return jax.shard_map(
        per_device,
        mesh=mesh,
        in_specs=placed,
        out_specs=(P(("dp", "neg"), None), P(("dp", "neg")), P(("neg", "dp"), None)),
        check_vma=False,
    )
```

```python
import functools
import jax
import jax.numpy as jnp
from jax import lax
from jax.experimental import pallas as pl
from jax.experimental.pallas import tpu as pltpu
from jax.sharding import PartitionSpec as P

LANES = 128
CHUNK = 512
SPLIT = 256
SPAN = 60.0
MIB = 1024 * 1024
FAR, NEAR = 2, 4
HALVING = ((3, 1), (1, 3))
LINE, RING, CORES = 4, 8, 2


def dot(a, b, dims):
    return lax.dot_general(a, b, (dims, ((), ())), preferred_element_type=jnp.float32)


def params(mib=16):
    return pltpu.CompilerParams(vmem_limit_bytes=mib * MIB)


def cost(flops, nbytes, exps):
    return pl.CostEstimate(flops=flops, bytes_accessed=nbytes, transcendentals=exps)


def mirror(value, bits=0):
    perm = []
    for l in range(LINE):
        for g in range(RING * CORES):
            for n in range(FAR * NEAR):
                to = ((LINE - 1 - l) * RING * CORES + g) * FAR * NEAR + (n ^ NEAR ^ bits)
                perm.append(((l * RING * CORES + g) * FAR * NEAR + n, to))
    return lax.ppermute(value, ("dp", "neg"), perm)


def swap_near(value, bits):
    perm = [(index, index ^ bits) for index in range(FAR * NEAR)]
    return lax.ppermute(value, "neg", perm)


def other_core(value):
    perm = [(index, index ^ 1) for index in range(LINE * RING * CORES)]
    return lax.ppermute(value, "dp", perm)


def lookup_kernel(
    place_ref, counts_ref, neg_ids_ref, pos_ids_ref, queries_ref, pos_ref, negatives_ref,
    corr_ref, score_ref, order_ref, tall_ref,
):
    counts = counts_ref[...].astype(jnp.float32)
    high = jnp.floor(counts * 0.125)
    digits = jnp.concatenate([high, counts - 8.0 * high], axis=1)
    table = digits.T.astype(jnp.bfloat16)
    table_rows = counts_ref.shape[0]
    total = negatives_ref.shape[0]
    block = total // (LINE * RING * CORES)
    place = place_ref[0]
    core = place & (CORES - 1)

    def corrections(ids):
        row = ids >> 7
        column = ids & (LANES - 1)
        width = ids.shape[1]
        spots = lax.broadcasted_iota(jnp.int32, (table_rows, width), 0)
        hot = jnp.where(spots == row, 1.0, 0.0).astype(jnp.bfloat16)
        found = dot(table, hot, ((1,), (0,)))
        value = 8.0 * found[:LANES] + found[LANES:]
        lanes = lax.broadcasted_iota(jnp.int32, (LANES, width), 0)
        picked = jnp.sum(jnp.where(lanes == column, value, 0.0), axis=0, keepdims=True)
        return jnp.log(picked)

    def target(index):
        l, r, c = index // (RING * CORES), (index // CORES) % RING, index % CORES
        away = (c - core) & (CORES - 1)
        return pl.ds(pl.multiple_of((away * LINE + l) * RING * block, block) + r * block, block)

    for k in range(neg_ids_ref.shape[0]):
        corr = corrections(neg_ids_ref[k : k + 1, :])
        tall = jnp.broadcast_to(corr, (LANES, LANES)).T
        for b in range(LANES // block):
            rows = target(k * (LANES // block) + b)
            tall_ref[rows, :] = tall[b * block : (b + 1) * block, :]
    for k in range(total // LANES):
        corr_ref[k : k + 1, :] = tall_ref[k * LANES : (k + 1) * LANES, :].T[:1, :]
    for k in range(total // block):
        order_ref[target(k), :] = negatives_ref[k * block : (k + 1) * block, :]
    products = queries_ref[...].astype(jnp.float32) * pos_ref[...].astype(jnp.float32)
    scores = jnp.sum(products.T, axis=0, keepdims=True)
    for k in range(pos_ids_ref.shape[0]):
        corr = corrections(pos_ids_ref[k : k + 1, :])
        lanes = slice(k * LANES, (k + 1) * LANES)
        score_ref[:, lanes] = scores[:, lanes] - corr


def wide(block, width):
    return jnp.concatenate([block] * (width // LANES), axis=1)


def row_stats(block, negatives_ref, corr_ref):
    rows = block.shape[0]
    top = None
    for start in range(0, negatives_ref.shape[0], CHUNK):
        part = slice(start, start + CHUNK)
        scores = dot(negatives_ref[part, :], block, ((1,), (1,)))
        scores = scores - wide(corr_ref[part, :], rows)
        tiles = scores.reshape(CHUNK // 8, 8, rows)
        best = jnp.max(tiles, axis=0)
        if top is None:
            top = best
            mass = jnp.sum(jnp.exp(tiles - top[None]), axis=0)
        else:
            new = jnp.maximum(top, best)
            mass = mass * jnp.exp(top - new) + jnp.sum(jnp.exp(tiles - new[None]), axis=0)
            top = new
    row_max = jnp.max(top, axis=0, keepdims=True)
    return row_max, jnp.sum(mass * jnp.exp(top - row_max), axis=0, keepdims=True)


def to_columns(rows_ref, out_ref):
    for k in range(rows_ref.shape[0]):
        tall = jnp.broadcast_to(rows_ref[k : k + 1, :], (LANES, LANES)).T
        out_ref[k * LANES : (k + 1) * LANES, :] = tall


def stats_kernel(
    spot_ref, blocks_hbm, negatives_ref, rows_ref, score_ref, out_ref, blocks_ref, corr_ref, sem
):
    fetch = pltpu.make_async_copy(blocks_hbm, blocks_ref, sem)
    fetch.start()
    to_columns(rows_ref, corr_ref)
    fetch.wait()
    score = score_ref[...]
    for side in range(FAR):
        for k in range(NEAR):
            row_max, row_sum = row_stats(blocks_ref[k, side], negatives_ref, corr_ref)
            if side == 0:
                own = spot_ref[0] == k
                joined = jnp.where(own, jnp.maximum(row_max, score), row_max)
                extra = jnp.exp(jnp.where(own, score, joined) - joined)
                row_sum = row_sum * jnp.exp(row_max - joined) + jnp.where(own, extra, 0.0)
                row_max = joined
            lse = row_max + jnp.log(row_sum)
            place = side * NEAR + k
            for c in range(NEAR):
                out_ref[c, place : place + 1, :] = lse


def join(parts):
    top = functools.reduce(jnp.maximum, parts)
    return top + jnp.log(sum(jnp.exp(part - top) for part in parts))


def join_kernel(parts_ref, out_ref):
    out_ref[...] = join([parts_ref[c] for c in range(NEAR)])


def grads_kernel(
    spot_ref, blocks_hbm, joined_ref, other_ref, negatives_ref, turned_ref, rows_ref, *refs
):
    query_outs, refs = refs[: 2 * FAR], refs[2 * FAR :]
    keep_out, send_out, lse_out, boost_ref, weight_ref, blocks_ref, corr_ref, sem = refs
    fetch = pltpu.make_async_copy(blocks_hbm, blocks_ref, sem)
    fetch.start()
    to_columns(rows_ref, corr_ref)
    total = negatives_ref.shape[0]
    spot = spot_ref[0]
    joined = joined_ref[...]
    other = jnp.concatenate([other_ref[NEAR:, :], other_ref[:NEAR, :]], axis=0)
    lse_all = join([joined, other])
    lse_out[...] = lse_all
    boost_ref[...] = jnp.exp(jnp.minimum(lse_all - joined, SPAN))
    half = total // CORES
    fetch.wait()
    for side in range(FAR):
        places = [spot ^ k for k in range(NEAR)]
        lse = [lse_out[pl.ds(side * NEAR + k, 1), :] for k in places]
        lse = jnp.concatenate(lse, axis=1)
        block = jnp.concatenate([blocks_ref[k, side] for k in places], axis=0)
        rows = block.shape[0]
        own = rows // NEAR
        for start in range(0, total, SPLIT):
            part = slice(start, start + SPLIT)
            scores = dot(negatives_ref[part, :], block, ((1,), (1,)))
            scores = scores - wide(corr_ref[part, :], rows)
            weight = jnp.exp(scores - lse).astype(jnp.bfloat16)
            weight_ref[part, :] = weight
            neg_term = dot(weight, block, ((1,), (0,)))
            which, place = start // half, slice(start % half, start % half + SPLIT)
            out = (keep_out, send_out)[which]
            if side > 0:
                neg_term = out[place, :] + neg_term
            out[place, :] = neg_term
        first, onward = HALVING[side]
        for index, k in enumerate(places):
            weight = weight_ref[:, index * own : (index + 1) * own]
            term = dot(turned_ref[...], weight, ((1,), (0,)))
            out = query_outs[side * 2 + (index in (first, first ^ onward))]
            place = int(index in (onward, first ^ onward))
            out[place] = term * boost_ref[pl.ds(side * NEAR + k, 1), :]


def spread_kernel(near_ref, far_ref, out_ref):
    for k in range(NEAR):
        out_ref[k, 0] = near_ref[...]
        out_ref[k, 1] = far_ref[...]


def sum_cores_kernel(keep_ref, got_ref, arrived_ref, out_ref):
    total = keep_ref[...] + got_ref[...]
    top = jnp.max(jnp.max(jnp.abs(total), axis=0, keepdims=True), axis=1, keepdims=True)
    power = jnp.clip(jnp.floor(jnp.log2(jnp.maximum(top, 1e-30))), -99.0, 99.0)
    scaled = total * jnp.exp2(13.0 - power)
    count, padded, width = out_ref.shape
    block = total.shape[0] // count
    for k in range(count):
        out_ref[k, :block, :] = scaled[k * block : (k + 1) * block, :]
        out_ref[k, block:, :] = jnp.broadcast_to(power, (padded - block, width))


def finish_kernel(
    spot_ref, near_ref, far_ref, pos_ref, score_ref, lse_ref, joined_ref, other_ref,
    neg_grad_ref, grad_ref, loss_ref,
):
    spot = spot_ref[0]
    lse = lse_ref[pl.ds(spot, 1), :]
    near_share = jnp.exp(-jnp.minimum(lse - joined_ref[pl.ds(spot, 1), :], SPAN))
    far_share = jnp.exp(-jnp.minimum(lse - other_ref[pl.ds(spot + NEAR, 1), :], SPAN))
    score = score_ref[...]
    pos_weight = jnp.exp(score - lse)
    turned = near_ref[...] * near_share + far_ref[...] * far_share
    turned = turned + (pos_weight - 1.0) * pos_ref[...].astype(jnp.float32).T
    grad_ref[...] = turned.T
    loss_ref[...] = lse - score


def trade(value, axis, groups):
    return lax.all_to_all(value, axis, 0, 0, tiled=True, axis_index_groups=groups)


def per_device(queries, positives, negatives, pos_ids, neg_ids, counts):
    own, width = queries.shape
    shard = negatives.shape[0]
    parts = FAR * NEAR
    f32, f16 = jnp.float32, jnp.float16
    like = jax.ShapeDtypeStruct
    place = lax.axis_index("dp").astype(jnp.int32).reshape(1)
    spot = (lax.axis_index("neg").astype(jnp.int32) % NEAR).reshape(1)
    smem = pl.BlockSpec(memory_space=pltpu.SMEM)
    vmem = pl.BlockSpec(memory_space=pltpu.VMEM)
    hbm = pl.BlockSpec(memory_space=pltpu.HBM)
    rows = [[f * NEAR + n for n in range(NEAR)] for f in range(FAR)]
    sheets = [[g * CORES + c for g in range(LINE * RING)] for c in range(CORES)]

    across = mirror(queries)

    corr, score, ordered = pl.pallas_call(
        lookup_kernel,
        in_specs=[smem] + [vmem] * 6,
        out_specs=(vmem, vmem, vmem),
        out_shape=(
            like((shard // LANES, LANES), f32),
            like((1, own), f32),
            like((shard, width), jnp.bfloat16),
        ),
        scratch_shapes=[pltpu.VMEM((shard, LANES), f32)],
        compiler_params=params(),
        cost_estimate=cost(10**9, 2 * 10**6, 4096),
        name="lookup",
    )(
        place,
        counts.reshape(-1, LANES),
        neg_ids.reshape(-1, LANES),
        pos_ids.reshape(-1, LANES),
        queries,
        positives,
        negatives,
    )
    turned = ordered.T

    blocks = pl.pallas_call(
        spread_kernel,
        in_specs=[vmem] * 2,
        out_specs=vmem,
        out_shape=like((NEAR, FAR, own, width), jnp.bfloat16),
        compiler_params=params(),
        name="spread",
    )(queries, across)
    blocks = trade(blocks, "neg", rows)

    pairs = parts * own * shard
    fetched = [
        pltpu.VMEM((NEAR, FAR, own, width), jnp.bfloat16),
        pltpu.VMEM((shard, LANES), f32),
        pltpu.SemaphoreType.DMA,
    ]
    stats = pl.pallas_call(
        stats_kernel,
        in_specs=[smem, hbm] + [vmem] * 3,
        out_specs=vmem,
        out_shape=like((NEAR, parts, own), f32),
        scratch_shapes=fetched,
        compiler_params=params(),
        cost_estimate=cost(2 * pairs * width, 4 * 10**6, pairs),
        name="stats",
    )(spot, blocks, ordered, corr, score)
    joined = pl.pallas_call(
        join_kernel,
        in_specs=[vmem],
        out_specs=vmem,
        out_shape=like((parts, own), f32),
        compiler_params=params(),
        name="join",
    )(trade(stats, "neg", rows))
    other = mirror(joined)

    near_keep, near_send, far_keep, far_send, keep, send, lse = pl.pallas_call(
        grads_kernel,
        in_specs=[smem, hbm] + [vmem] * 5,
        out_specs=(vmem,) * (2 * FAR + 3),
        out_shape=(
            *[like((2, width, own), f32)] * (2 * FAR),
            like((shard // CORES, width), f32),
            like((shard // CORES, width), f32),
            like((parts, own), f32),
        ),
        scratch_shapes=[
            pltpu.VMEM((parts, own), f32),
            pltpu.VMEM((shard, NEAR * own), jnp.bfloat16),
            *fetched,
        ],
        compiler_params=params(24),
        cost_estimate=cost(6 * pairs * width, 8 * 10**6, pairs),
        name="grads",
    )(spot, blocks, joined, other, ordered, turned, corr)
    from_core = other_core(send)

    far_got = swap_near(far_send.astype(f16), HALVING[1][0])
    near_got = swap_near(near_send.astype(f16), HALVING[0][0])
    arrived = near_got[0, :8, :LANES].astype(f32) + far_got[0, :8, :LANES].astype(f32)
    far_sums = (far_keep + far_got.astype(f32)).astype(f16)
    query_far = mirror(far_sums[0]).astype(f32) + mirror(far_sums[1], HALVING[1][1]).astype(f32)
    onward = (near_keep[1] + near_got[1].astype(f32)).astype(f16)
    near_acc = near_keep[0] + near_got[0].astype(f32)
    near_acc = near_acc + swap_near(onward, HALVING[0][1]).astype(f32)

    count = LINE * RING
    block = shard // CORES // count
    neg_acc = pl.pallas_call(
        sum_cores_kernel,
        in_specs=[vmem] * 3,
        out_specs=vmem,
        out_shape=like((count, block + 8, width), f32),
        compiler_params=params(),
        cost_estimate=cost(10**6, 10**6, 0),
        name="sum_cores",
    )(keep, from_core, arrived)
    neg_acc = trade(neg_acc.astype(f16), "dp", sheets).astype(f32)
    power = jnp.exp2(neg_acc[:, block : block + 1, :1] - 13.0)
    neg_grad = jnp.sum(neg_acc[:, :block, :] * power, axis=0)

    query_grad, row_loss = pl.pallas_call(
        finish_kernel,
        in_specs=[smem] + [vmem] * 7 + [hbm],
        out_specs=(vmem, vmem),
        out_shape=(like((own, width), f32), like((1, own), f32)),
        compiler_params=params(),
        name="finish",
    )(spot, near_acc, query_far, positives, score, lse, joined, other, neg_grad)
    return (query_grad, row_loss.reshape(own), neg_grad)


def solution(mesh):
    placed = (
        P(("dp", "neg"), None),
        P(("dp", "neg"), None),
        P("neg", None),
        P(("dp", "neg")),
        P("neg"),
        P(),
    )
    return jax.shard_map(
        per_device,
        mesh=mesh,
        in_specs=placed,
        out_specs=(P(("dp", "neg"), None), P(("dp", "neg")), P(("neg", "dp"), None)),
        check_vma=False,
    )
```
